32 devices in a mesh: seq: 8 (over z, y), chan: 4 (over x, core).
Axes of the slice: x: 2, y: 2, z: 4, core: 2. Of those that a mesh axis runs over, the one named last changes fastest.
Arguments:
- tokens: bfloat16 [8192, 512], P('seq', 'chan'), may hold values from -6 to 6
- w_in: bfloat16 [512, 3, 512], P(None, None, 'chan'), may hold values from -0.25 to 0.25
- short_filter: float32 [3, 3, 512], P(None, None, 'chan'), may hold values from -3 to 3
- long_filter: float32 [8192, 512], P('seq', 'chan'), may hold values from -0.0625 to 0.0625
- skip_gain: float32 [512], P('chan'), may hold values from 0.5 to 1.5
- w_out: bfloat16 [512, 512], P('chan'), may hold values from -0.25 to 0.25
Outputs:
- mixed: bfloat16 [8192, 512], P('seq', 'chan')
The draws below stay inside these ranges and needn't reach their ends.
All inputs are finite; a program needn't handle non-finite values.
Results may differ from the reference program's by a relative error of at most 0.007.
Values may be sent and summed in bfloat16 or wider, within the bound.
A program may use at most 64 MiB of HBM per device.

```python
import jax
import jax.numpy as jnp

C = 512
L = 8192


def block_scale(rng, dims, shards, low, high):
    def one(dim, shards_of):
        steps = jax.random.uniform(jax.random.fold_in(jax.random.fold_in(rng, 6), dim), (shards_of,), jnp.float32, low / len(shards), high / len(shards))
        return jnp.repeat(jnp.exp(steps), dims[dim] // shards_of).reshape((-1,) + (1,) * (len(dims) - dim - 1))

    factor_of = one(*shards[0])
    for cut in shards[1:]:
        factor_of = factor_of * one(*cut)
    return factor_of


def scatter_about(own_key, dims, scale, limit, shards=(), kind=jnp.bfloat16):
    loudness = block_scale(own_key, dims, shards, -0.22, 0.18) if shards else 1.0
    drawn = jax.random.normal(own_key, dims, jnp.float32) * scale * loudness
    return jnp.minimum(jnp.maximum(drawn, -limit), limit).astype(kind)


def setup_inputs(seed: int = 0) -> dict:
    splits = jax.random.split(jax.random.key(seed), 7)
    tokens = scatter_about(splits[0], (L, C), 1.0, 6.0, ((0, 8), (1, 4)))
    w_in = scatter_about(splits[1], (C, 3, C), C ** -0.5, 0.25, ((2, 4),))
    short_filter = scatter_about(splits[2], (3, 3, C), 0.6, 3.0, ((2, 4),), jnp.float32)
    long_filter = scatter_about(splits[3], (L, C), L ** -0.5, 0.0625, ((0, 8), (1, 4)), jnp.float32)
    skip_gain = jnp.clip(0.5 + 1.0 * jax.random.uniform(splits[4], (C,), jnp.float32) ** block_scale(splits[4], (C,), ((0, 4),), -0.2, 0.2), 0.5, 1.5)
    w_out = scatter_about(splits[5], (C, C), C ** -0.5, 0.25, ((0, 4),))
    return {"tokens": tokens, "w_in": w_in, "short_filter": short_filter, "long_filter": long_filter, "skip_gain": skip_gain, "w_out": w_out}


def reference(tokens, w_in, short_filter, long_filter, skip_gain, w_out):
    width = tokens.shape[1]
    length = tokens.shape[0]
    projected = jnp.dot(tokens, w_in.reshape(width, 3 * width), preferred_element_type=jnp.float32)
    projected = projected.astype(jnp.bfloat16).reshape(length, 3, width)
    padded = jnp.concatenate([jnp.zeros((2, 3, width), jnp.float32), projected.astype(jnp.float32)], axis=0)
    short = short_filter[0] * padded[2:] + short_filter[1] * padded[1:-1] + short_filter[2] * padded[:-2]
    inner = short[:, 0, :] * short[:, 1, :]
    spectrum = jnp.fft.rfft(inner, n=2 * length, axis=0) * jnp.fft.rfft(long_filter, n=2 * length, axis=0)
    conv = jnp.fft.irfft(spectrum, n=2 * length, axis=0)[:length]
    gated = (short[:, 2, :] * (conv + skip_gain * inner)).astype(jnp.bfloat16)
    return jnp.dot(gated, w_out, preferred_element_type=jnp.float32).astype(jnp.bfloat16)
```

```python
import functools
import math

import jax
import jax.numpy as jnp
import numpy as np
from jax import lax
from jax.experimental import pallas as pl
from jax.experimental.pallas import tpu as pltpu
from jax.sharding import PartitionSpec as P

MESH = pl.DeviceIdType.MESH
LANES = 128
RIM = 16
F32 = jnp.float32
BF16 = jnp.bfloat16


def split(values):
    high = values.astype(BF16)
    low = (values - high.astype(F32)).astype(BF16)
    return high, low


def split_table(table):
    table = np.asarray(table, np.float64)
    high = table.astype(np.float32).astype(BF16)
    low = (table - high.astype(np.float64)).astype(np.float32).astype(BF16)
    return high, low


def tables(total):
    first = total // LANES
    half = first // 2
    kept = half + 1
    padded = -(-kept // 16) * 16
    k1 = np.arange(padded)
    live = (k1 < kept).astype(np.float64)[:, None]
    n1 = np.arange(half)
    angle = 2.0 * math.pi / first * (k1[:, None] * n1[None, :] % first)
    outer = np.concatenate([np.cos(angle) * live, -np.sin(angle) * live], axis=0)
    outer_high, outer_low = split_table(outer)
    outer_table = np.concatenate([outer_high, outer_low], axis=1)
    n2 = np.arange(LANES)
    turn = 2.0 * math.pi / total * (k1[:, None] * n2[None, :] % total)
    turn_table = np.stack([np.cos(turn), -np.sin(turn)]).astype(np.float32)
    inner = 2.0 * math.pi / LANES * (n2[:, None] * n2[None, :] % LANES)
    cosine, sine = np.cos(inner), -np.sin(inner)
    ahead = np.block([[cosine, sine], [-sine, cosine]])
    ahead_table = np.stack(split_table(ahead))
    back_table = np.stack(split_table(ahead.T))
    weight = np.where((k1 == 0) | (k1 == half), 1.0, 2.0) * live[:, 0] / total
    close = np.concatenate([np.cos(angle).T * weight, -np.sin(angle).T * weight], axis=1)
    close_table = np.stack(split_table(close))
    return outer_table, turn_table, ahead_table, back_table, close_table


def dot(left, right):
    return jnp.dot(left, right, preferred_element_type=F32)


def dot3(left, table_ref):
    high, low = split(left)
    return dot(high, table_ref[0]) + (dot(low, table_ref[0]) + dot(high, table_ref[1]))


def kernel(
    shards, chans, chunks, group,
    tok, w_in, sfilt, lfilt, gain, w_out, outer_t, turn_t, ahead_t, back_t, close_t,
    out,
    tbuf, proj, rim_out, rim_in, keep, inner_s, stage, hs, hr, xs, xr, ys, yr,
    x32, h32, y32, cscr, gbuf, wbuf,
    tok_send, tok_recv, fwd_send, wo_send, wo_recv, rim_send, rim_recv,
    h_send, h_recv, x_send, x_recv, y_send, y_recv, g_send, g_recv, gf_send,
):
    seq = lax.axis_index("seq")
    chan = lax.axis_index("chan")
    count = tok.shape[0]
    blocks = count // LANES
    cd = LANES // shards
    half_rows = blocks // 2 * cd
    rows = count // chunks
    core_peer = chan + 1 - 2 * (chan % 2)
    x_peer = (chan + 2) % chans
    diag = (core_peer + 2) % chans
    others = (core_peer, x_peer, diag)

    barrier = pltpu.get_barrier_semaphore()
    for peer in others:
        pl.semaphore_signal(barrier, inc=1, device_id=(seq, peer), device_id_type=MESH)

    def greet(d, carry):
        peer = (seq + d) % shards
        pl.semaphore_signal(barrier, inc=1, device_id=(peer, chan), device_id_type=MESH)
        return carry

    lax.fori_loop(1, shards, greet, 0)
    pl.semaphore_wait(barrier, len(others) + shards - 1)

    def remote(src, dst, send, recv, device):
        return pltpu.make_async_remote_copy(
            src_ref=src, dst_ref=dst, send_sem=send, recv_sem=recv,
            device_id=device, device_id_type=MESH,
        )

    order = [chunks - 1] + list(range(chunks - 1))

    def tok_copy(k, slot, peer, owner):
        span = pl.ds(k * rows, rows)
        return remote(tok.at[span], tbuf.at[owner, span], tok_send.at[slot, k], tok_recv.at[owner, k], (seq, peer))

    def fwd_copy(k, owner):
        span = pl.ds(k * rows, rows)
        return remote(tbuf.at[owner, span], tbuf.at[owner, span], fwd_send.at[k], tok_recv.at[owner, k], (seq, core_peer))

    for k in order:
        tok_copy(k, 1, x_peer, chan).start()
        tok_copy(k, 0, core_peer, chan).start()

    def wo_copy(slot, peer, owner):
        columns = pl.ds(pl.multiple_of(peer * LANES, LANES), LANES)
        return remote(w_out.at[:, columns], wbuf.at[owner], wo_send.at[slot], wo_recv.at[owner], (seq, peer))

    def swap(src, dst, send, recv, half, peer, owner):
        span = pl.ds(half * half_rows, half_rows)
        return remote(src.at[peer, span], dst.at[owner, span], send.at[half, peer], recv.at[half, owner], (peer, chan))

    def swap_start(src, dst, send, recv, half):
        def one(d, carry):
            swap(src, dst, send, recv, half, (seq + d) % shards, seq).start()
            return carry
        lax.fori_loop(1, shards, one, 0)

    def swap_wait_recv(src, dst, send, recv, half):
        def one(d, carry):
            peer = (seq + d) % shards
            swap(src, dst, send, recv, half, peer, peer).wait_recv()
            return carry
        lax.fori_loop(1, shards, one, 0)

    def swap_wait_send(src, dst, send, recv, half):
        def one(d, carry):
            swap(src, dst, send, recv, half, (seq + d) % shards, seq).wait_send()
            return carry
        lax.fori_loop(1, shards, one, 0)

    def spread(values, block):
        turned = values.T
        for dest in range(shards):
            stage[dest, block * cd:(block + 1) * cd, :] = turned[dest * cd:(dest + 1) * cd, :]

    def pack(dst, half):
        span = slice(half * half_rows, (half + 1) * half_rows)
        dst[:, span, :] = stage[:, span, :].astype(BF16)

    for half in range(2):
        for block in range(half * blocks // 2, (half + 1) * blocks // 2):
            spread(lfilt[block * LANES:(block + 1) * LANES, :], block)
        pack(hs, half)
        swap_start(hs, hr, h_send, h_recv, half)
    hr[seq] = hs[seq]

    for slot, peer in enumerate(others):
        wo_copy(slot, peer, chan).start()
    wbuf[chan] = w_out[:, pl.ds(pl.multiple_of(chan * LANES, LANES), LANES)]
    tbuf[chan] = tok[...]

    def shorten(k):
        for g in range(3):
            lanes = slice(g * LANES, (g + 1) * LANES)
            base = RIM + k * rows
            value = (
                sfilt[0, g:g + 1, :] * proj[base:base + rows, lanes]
                + sfilt[1, g:g + 1, :] * proj[base - 1:base - 1 + rows, lanes]
                + sfilt[2, g:g + 1, :] * proj[base - 2:base - 2 + rows, lanes]
            )
            if g == 0:
                held = value
            elif g == 1:
                held = held * value
                inner_s[k * rows:(k + 1) * rows, :] = held
            else:
                keep[k * rows:(k + 1) * rows, :] = value
        for j in range(rows // LANES):
            spread(held[j * LANES:(j + 1) * LANES, :], k * (rows // LANES) + j)

    def rim_copy():
        return remote(rim_out, rim_in, rim_send, rim_recv, ((seq + 1) % shards, chan))

    for place, k in enumerate(order):
        tok_copy(k, 1, x_peer, x_peer).wait_recv()
        fwd_copy(k, x_peer).start()
        tok_copy(k, 0, core_peer, core_peer).wait_recv()
        tok_copy(k, 0, core_peer, diag).wait_recv()
        features = jnp.concatenate([tbuf[j, k * rows:(k + 1) * rows, :] for j in range(chans)], axis=1)
        projected = dot(features, w_in[...]).astype(BF16)
        proj[RIM + k * rows:RIM + (k + 1) * rows, :] = projected.astype(F32)
        if place == 0:
            rim_out[...] = projected[rows - RIM:, :]
            rim_copy().start()
        else:
            if place == 1:
                rim_copy().wait_recv()
                live = (seq > 0).astype(F32)
                proj[0:RIM, :] = rim_in[...].astype(F32) * live
            shorten(k)
            if (k + 1) * 2 == chunks:
                pack(xs, 0)
                swap_start(xs, xr, x_send, x_recv, 0)
    shorten(chunks - 1)
    pack(xs, 1)
    swap_start(xs, xr, x_send, x_recv, 1)
    xr[seq] = xs[seq]

    for half in range(2):
        swap_wait_recv(hs, hr, h_send, h_recv, half)
    h32[...] = hr[...].reshape(h32.shape).astype(F32)
    for half in range(2):
        swap_wait_recv(xs, xr, x_send, x_recv, half)
    x32[...] = xr[...].reshape(x32.shape).astype(F32)

    height = shards * blocks
    padded = turn_t.shape[1]

    def channels(i, carry):
        columns = []
        for ref in (x32, h32):
            for j in range(group):
                columns.append(ref[pl.ds(i * group + j, height, stride=cd), :].astype(BF16))
        signal = jnp.concatenate(columns, axis=1)
        signal = jnp.concatenate([signal, signal], axis=0)
        opened = dot(outer_t[...], signal)
        cosine, sine = turn_t[0], turn_t[1]
        turned = []
        for j in range(2 * group):
            real = opened[:padded, j * LANES:(j + 1) * LANES]
            imag = opened[padded:, j * LANES:(j + 1) * LANES]
            turned.append(jnp.concatenate([real * cosine - imag * sine, real * sine + imag * cosine], axis=1))
        spectra = dot3(jnp.concatenate(turned, axis=0), ahead_t)
        edge = group * padded
        xr_, xi_ = spectra[:edge, :LANES], spectra[:edge, LANES:]
        hr_, hi_ = spectra[edge:, :LANES], spectra[edge:, LANES:]
        product = jnp.concatenate([xr_ * hr_ - xi_ * hi_, xr_ * hi_ + xi_ * hr_], axis=1)
        back = dot3(product, back_t)
        sums = []
        for j in range(group):
            real = back[j * padded:(j + 1) * padded, :LANES]
            imag = back[j * padded:(j + 1) * padded, LANES:]
            sums.append(jnp.concatenate([real * cosine + imag * sine, imag * cosine - real * sine], axis=0))
        closing = jnp.concatenate(sums, axis=1)
        high, low = split(closing)
        conv = dot(close_t[0], high) + (dot(close_t[0], low) + dot(close_t[1], high))
        for j in range(group):
            y32[pl.ds(i * group + j, height, stride=cd), :] = conv[:, j * LANES:(j + 1) * LANES]
        return carry

    lax.fori_loop(0, cd // group, channels, 0)

    ys[...] = y32[...].astype(BF16).reshape(ys.shape)
    for half in range(2):
        swap_start(ys, yr, y_send, y_recv, half)
    yr[seq] = ys[seq]

    def gated_copy(half, slot, peer, owner):
        span = pl.ds(half * (count // 2), count // 2)
        return remote(gbuf.at[chan, span], gbuf.at[owner, span], g_send.at[slot, half], g_recv.at[owner, half], (seq, peer))

    def gated_fwd(half, owner):
        span = pl.ds(half * (count // 2), count // 2)
        return remote(gbuf.at[owner, span], gbuf.at[owner, span], gf_send.at[half], g_recv.at[owner, half], (seq, core_peer))

    for half in range(2):
        swap_wait_recv(ys, yr, y_send, y_recv, half)
        for src in range(shards):
            span = slice(half * half_rows, (half + 1) * half_rows)
            piece = yr[src, span, :].astype(F32)
            for j in range(blocks // 2):
                cscr[half * (blocks // 2) + j, src * cd:(src + 1) * cd, :] = piece[j * cd:(j + 1) * cd, :]
        for block in range(half * blocks // 2, (half + 1) * blocks // 2):
            span = slice(block * LANES, (block + 1) * LANES)
            conv = cscr[block].T
            gated = keep[span, :] * (conv + gain[...] * inner_s[span, :])
            gbuf[chan, span, :] = gated.astype(BF16)
        gated_copy(half, 1, x_peer, chan).start()
        gated_copy(half, 0, core_peer, chan).start()

    for slot, peer in enumerate(others):
        wo_copy(slot, peer, peer).wait_recv()
    weights = jnp.concatenate([wbuf[j] for j in range(chans)], axis=0)
    for half in range(2):
        gated_copy(half, 1, x_peer, x_peer).wait_recv()
        gated_fwd(half, x_peer).start()
    for half in range(2):
        gated_copy(half, 0, core_peer, core_peer).wait_recv()
        gated_copy(half, 0, core_peer, diag).wait_recv()
        span = slice(half * (count // 2), (half + 1) * (count // 2))
        whole = jnp.concatenate([gbuf[j, span, :] for j in range(chans)], axis=1)
        out[span, :] = dot(whole, weights).astype(BF16)

    for k in range(chunks):
        tok_copy(k, 1, x_peer, chan).wait_send()
        tok_copy(k, 0, core_peer, chan).wait_send()
        fwd_copy(k, x_peer).wait_send()
    for slot, peer in enumerate(others):
        wo_copy(slot, peer, chan).wait_send()
    rim_copy().wait_send()
    for half in range(2):
        swap_wait_send(hs, hr, h_send, h_recv, half)
        swap_wait_send(xs, xr, x_send, x_recv, half)
        swap_wait_send(ys, yr, y_send, y_recv, half)
        gated_copy(half, 1, x_peer, chan).wait_send()
        gated_copy(half, 0, core_peer, chan).wait_send()
        gated_fwd(half, x_peer).wait_send()


def on_device(shards, chans, tokens, w_in, short_filter, long_filter, skip_gain, w_out):
    count, width = tokens.shape
    length = shards * count
    blocks = count // LANES
    cd = width // shards
    chunks = 4
    group = min(cd, 4)
    consts = tables(2 * length)
    wide = 3 * width
    dma = pltpu.SemaphoreType.DMA
    swap_shape = (shards, blocks * cd, LANES)
    flat_shape = (shards * blocks * cd, LANES)
    vmem = pl.BlockSpec(memory_space=pltpu.VMEM)
    operands = (
        tokens, w_in.reshape(w_in.shape[0], wide), short_filter, long_filter,
        skip_gain.reshape(1, width), w_out,
    ) + tuple(jnp.asarray(c) for c in consts)
    return pl.pallas_call(
        functools.partial(kernel, shards, chans, chunks, group),
        out_shape=jax.ShapeDtypeStruct((count, width), BF16),
        in_specs=[vmem] * len(operands),
        out_specs=vmem,
        scratch_shapes=[
            pltpu.VMEM((chans, count, width), BF16),
            pltpu.VMEM((RIM + count, wide), F32),
            pltpu.VMEM((RIM, wide), BF16),
            pltpu.VMEM((RIM, wide), BF16),
            pltpu.VMEM((count, width), F32),
            pltpu.VMEM((count, width), F32),
            pltpu.VMEM(swap_shape, F32),
            pltpu.VMEM(swap_shape, BF16),
            pltpu.VMEM(swap_shape, BF16),
            pltpu.VMEM(swap_shape, BF16),
            pltpu.VMEM(swap_shape, BF16),
            pltpu.VMEM(swap_shape, BF16),
            pltpu.VMEM(swap_shape, BF16),
            pltpu.VMEM(flat_shape, F32),
            pltpu.VMEM(flat_shape, F32),
            pltpu.VMEM(flat_shape, F32),
            pltpu.VMEM((blocks, LANES, LANES), F32),
            pltpu.VMEM((chans, count, width), BF16),
            pltpu.VMEM((chans, width, LANES), BF16),
            dma((2, chunks)), dma((chans, chunks)), dma((chunks,)),
            dma((3,)), dma((chans,)), dma, dma,
            dma((2, shards)), dma((2, shards)),
            dma((2, shards)), dma((2, shards)),
            dma((2, shards)), dma((2, shards)),
            dma((2, 2)), dma((chans, 2)), dma((2,)),
        ],
        compiler_params=pltpu.CompilerParams(
            collective_id=0, has_side_effects=True, vmem_limit_bytes=48 * 1024 * 1024
        ),
        cost_estimate=pl.CostEstimate(flops=4 * 10**9, bytes_accessed=4 * 10**6, transcendentals=0),
    )(*operands)


def solution(mesh):
    shards, chans = mesh.shape["seq"], mesh.shape["chan"]
    return jax.shard_map(
        functools.partial(on_device, shards, chans),
        mesh=mesh,
        in_specs=(
            P("seq", "chan"),
            P(None, None, "chan"),
            P(None, None, "chan"),
            P("seq", "chan"),
            P("chan"),
            P("chan", None),
        ),
        out_specs=P("seq", "chan"),
        check_vma=False,
    )
```

```python
import functools
import math

import jax
import jax.numpy as jnp
import numpy as np
from jax import lax
from jax.experimental import pallas as pl
from jax.experimental.pallas import tpu as pltpu
from jax.sharding import PartitionSpec as P

MESH = pl.DeviceIdType.MESH
LANES = 128
RIM = 16
F32 = jnp.float32
BF16 = jnp.bfloat16


def split(values):
    high = values.astype(BF16)
    low = (values - high.astype(F32)).astype(BF16)
    return high, low


def split_table(table):
    table = np.asarray(table, np.float64)
    high = table.astype(np.float32).astype(BF16)
    low = (table - high.astype(np.float64)).astype(np.float32).astype(BF16)
    return high, low


def tables(total):
    first = total // LANES
    half = first // 2
    kept = half + 1
    padded = -(-kept // 16) * 16
    k1 = np.arange(padded)
    live = (k1 < kept).astype(np.float64)[:, None]
    n1 = np.arange(half)
    angle = 2.0 * math.pi / first * (k1[:, None] * n1[None, :] % first)
    outer = np.concatenate([np.cos(angle) * live, -np.sin(angle) * live], axis=0)
    outer_table = np.concatenate(split_table(outer), axis=1).astype(np.float32)
    n2 = np.arange(LANES)
    turn = 2.0 * math.pi / total * (k1[:, None] * n2[None, :] % total)
    turn_table = np.stack([np.cos(turn), -np.sin(turn)]).astype(np.float32)
    inner = 2.0 * math.pi / LANES * (n2[:, None] * n2[None, :] % LANES)
    cosine, sine = np.cos(inner), -np.sin(inner)
    ahead = np.block([[cosine, sine], [-sine, cosine]])
    ahead_table = ahead.astype(np.float32)
    back_table = ahead.T.astype(np.float32)
    weight = np.where((k1 == 0) | (k1 == half), 1.0, 2.0) * live[:, 0] / total
    close = np.concatenate([np.cos(angle).T * weight, -np.sin(angle).T * weight], axis=1)
    close_table = close.astype(np.float32)
    return outer_table, turn_table, ahead_table, back_table, close_table


def dot(left, right):
    return jnp.dot(left, right, preferred_element_type=F32)


def dot3(left, table_ref):
    high, low = split(left)
    return dot(high, table_ref[0]) + (dot(low, table_ref[0]) + dot(high, table_ref[1]))


def kernel(
    shards, chans, chunks, parts, group,
    tok, w_in, sfilt_a, lfilt_a, gain_a, w_out, outer_a, turn_a, ahead_a, back_a, close_a,
    out,
    tbuf, tmini, w, sfilt, lfilt, gain, outer_f, turn_t, ahead_f, back_f, close_f,
    outer_t, ahead_t, back_t, close_t,
    proj, rim_out, rim_in, keep, keep_t, skip_t, stage, hs, hr, xs, xr, ys, yr,
    x32, h32, hspec, y32, c32, gbuf, wbuf, w32, wt, acc,
    local, tok_send, tok_recv, fwd_send, wo_send, wo_recv, rim_send, rim_recv,
    h_send, h_recv, x_send, x_recv, y_send, y_recv, g_send, g_recv, gf_send,
):
    seq = lax.axis_index("seq")
    chan = lax.axis_index("chan")
    count = tok.shape[0]
    blocks = count // LANES
    cd = LANES // shards
    groups = cd // group
    rows = count // chunks
    core_peer = chan + 1 - 2 * (chan % 2)
    x_peer = (chan + 2) % chans
    diag = (core_peer + 2) % chans
    others = (core_peer, x_peer, diag)

    own_columns = pl.ds(pl.multiple_of(chan * LANES, LANES), LANES)
    loads = [(lfilt_a, lfilt), (tok, tbuf.at[chan]), (tok.at[pl.ds(count - RIM, RIM)], tmini.at[chan])]
    loads += [(w_in.at[g], w.at[:, pl.ds(g * LANES, LANES)]) for g in range(3)]
    loads += [(sfilt_a, sfilt), (gain_a, gain), (w_out.at[:, own_columns], wbuf.at[chan])]
    loads += [(outer_a, outer_f), (turn_a, turn_t), (ahead_a, ahead_f), (back_a, back_f), (close_a, close_f)]
    copies = [pltpu.make_async_copy(src, dst, local.at[i]) for i, (src, dst) in enumerate(loads)]
    for copy in copies:
        copy.start()

    barrier = pltpu.get_barrier_semaphore()
    for peer in others:
        pl.semaphore_signal(barrier, inc=1, device_id=(seq, peer), device_id_type=MESH)

    def greet(d, carry):
        peer = (seq + d) % shards
        pl.semaphore_signal(barrier, inc=1, device_id=(peer, chan), device_id_type=MESH)
        return carry

    lax.fori_loop(1, shards, greet, 0)
    pl.semaphore_wait(barrier, len(others) + shards - 1)

    def remote(src, dst, send, recv, device):
        return pltpu.make_async_remote_copy(
            src_ref=src, dst_ref=dst, send_sem=send, recv_sem=recv,
            device_id=device, device_id_type=MESH,
        )

    def landing(k, owner):
        if k == 0:
            return tmini.at[owner]
        return tbuf.at[owner, pl.ds((k - 1) * rows, rows)]

    def tok_copy(k, slot, peer, owner):
        span = pl.ds(count - RIM, RIM) if k == 0 else pl.ds((k - 1) * rows, rows)
        return remote(tok.at[span], landing(k, owner), tok_send.at[slot, k], tok_recv.at[owner, k], (seq, peer))

    def fwd_copy(k, owner):
        return remote(landing(k, owner), landing(k, owner), fwd_send.at[k], tok_recv.at[owner, k], (seq, core_peer))

    for k in range(chunks + 1):
        tok_copy(k, 1, x_peer, chan).start()
        tok_copy(k, 0, core_peer, chan).start()

    def wo_copy(slot, peer, owner):
        columns = pl.ds(pl.multiple_of(peer * LANES, LANES), LANES)
        return remote(w_out.at[:, columns], wbuf.at[owner], wo_send.at[slot], wo_recv.at[owner], (seq, peer))

    def swap(src, dst, send, recv, part, span, peer, owner):
        return remote(src.at[peer, span], dst.at[owner, span], send.at[part, peer], recv.at[part, owner], (peer, chan))

    def swap_all(action, src, dst, send, recv, part, span):
        def one(d, carry):
            peer = (seq + d) % shards
            if action == "start":
                swap(src, dst, send, recv, part, span, peer, seq).start()
            elif action == "recv":
                swap(src, dst, send, recv, part, span, peer, peer).wait_recv()
            else:
                swap(src, dst, send, recv, part, span, peer, seq).wait_send()
            return carry
        lax.fori_loop(1, shards, one, 0)

    def h_swap(action, half):
        size = blocks // 2 * cd
        swap_all(action, hs, hr, h_send, h_recv, half, pl.ds(half * size, size))

    def x_swap(action, part):
        size = blocks // parts * cd
        swap_all(action, xs, xr, x_send, x_recv, part, pl.ds(part * size, size))

    def y_swap(action, g):
        swap_all(action, ys.at[g], yr.at[g], y_send, y_recv, g, pl.ds(0, group * blocks))

    def spread(turned, block):
        for dest in range(shards):
            stage[dest, block * cd:(block + 1) * cd, :] = turned[dest * cd:(dest + 1) * cd, :]

    def pack(dst, part, pieces):
        size = blocks // pieces * cd
        span = slice(part * size, (part + 1) * size)
        dst[:, span, :] = stage[:, span, :].astype(BF16)

    copies[0].wait()
    for half in range(2):
        for block in range(half * blocks // 2, (half + 1) * blocks // 2):
            spread(lfilt[block * LANES:(block + 1) * LANES, :].T, block)
        pack(hs, half, 2)
        h_swap("start", half)
    hr[seq] = hs[seq]
    for slot, peer in enumerate(others):
        wo_copy(slot, peer, chan).start()
    for copy in copies[1:]:
        copy.wait()
    gain_rows = jnp.broadcast_to(gain[...], (LANES, LANES)).T

    def shorten(k):
        for g in range(3):
            lanes = slice(g * LANES, (g + 1) * LANES)
            base = RIM + k * rows
            value = (
                sfilt[0, g:g + 1, :] * proj[base:base + rows, lanes]
                + sfilt[1, g:g + 1, :] * proj[base - 1:base - 1 + rows, lanes]
                + sfilt[2, g:g + 1, :] * proj[base - 2:base - 2 + rows, lanes]
            )
            if g == 0:
                held = value
            elif g == 1:
                held = held * value
            else:
                keep[k * rows:(k + 1) * rows, :] = value
        for j in range(rows // LANES):
            block = k * (rows // LANES) + j
            turned = held[j * LANES:(j + 1) * LANES, :].T
            spread(turned, block)
            skip_t[block * LANES:(block + 1) * LANES, :] = turned * gain_rows

    def rim_copy():
        return remote(rim_out, rim_in, rim_send, rim_recv, ((seq + 1) % shards, chan))

    def take(k):
        tok_copy(k, 1, x_peer, x_peer).wait_recv()
        fwd_copy(k, x_peer).start()
        tok_copy(k, 0, core_peer, core_peer).wait_recv()
        tok_copy(k, 0, core_peer, diag).wait_recv()

    take(0)
    tail = jnp.concatenate([tmini[j] for j in range(chans)], axis=1)
    rim_out[...] = dot(tail, w[...]).astype(BF16)
    rim_copy().start()
    outer_t[...] = outer_f[...].astype(BF16)
    for table, ref in ((ahead_f, ahead_t), (back_f, back_t), (close_f, close_t)):
        high, low = split(table[...])
        ref[0] = high
        ref[1] = low
    for k in range(chunks):
        take(k + 1)
        features = jnp.concatenate([tbuf[j, k * rows:(k + 1) * rows, :] for j in range(chans)], axis=1)
        projected = dot(features, w[...]).astype(BF16)
        proj[RIM + k * rows:RIM + (k + 1) * rows, :] = projected.astype(F32)
        if k == 0:
            rim_copy().wait_recv()
            live = (seq > 0).astype(F32)
            proj[0:RIM, :] = rim_in[...].astype(F32) * live
        shorten(k)
        if (k + 1) * parts % chunks == 0:
            part = (k + 1) * parts // chunks - 1
            pack(xs, part, parts)
            x_swap("start", part)
    xr[seq] = xs[seq]

    height = shards * blocks
    padded = turn_t.shape[1]
    edge = group * padded

    def spectrum(ref, g):
        columns = [ref[pl.ds(g * group + j, height, stride=cd), :].astype(BF16) for j in range(group)]
        signal = jnp.concatenate(columns, axis=1)
        signal = jnp.concatenate([signal, signal], axis=0)
        opened = dot(outer_t[...], signal)
        cosine, sine = turn_t[0], turn_t[1]
        turned = []
        for j in range(group):
            real = opened[:padded, j * LANES:(j + 1) * LANES]
            imag = opened[padded:, j * LANES:(j + 1) * LANES]
            turned.append(jnp.concatenate([real * cosine - imag * sine, real * sine + imag * cosine], axis=1))
        return dot3(jnp.concatenate(turned, axis=0), ahead_t)

    for half in range(2):
        h_swap("recv", half)
    h32[...] = hr[...].reshape(h32.shape).astype(F32)
    for g in range(groups):
        hspec[g] = spectrum(h32, g)
    for block in range(blocks):
        span = slice(block * LANES, (block + 1) * LANES)
        keep_t[span, :] = keep[span, :].T
    for slot, peer in enumerate(others):
        wo_copy(slot, peer, peer).wait_recv()
    for j in range(chans):
        w32[...] = wbuf[j].astype(F32)
        for g in range(groups):
            picked = [w32[pl.ds(g * group + c, shards, stride=cd), :] for c in range(group)]
            wt[g, j] = jnp.concatenate(picked, axis=0).astype(BF16)

    for part in range(parts):
        x_swap("recv", part)
    x32[...] = xr[...].reshape(x32.shape).astype(F32)

    def convolve(g):
        spectra = spectrum(x32, g)
        xr_, xi_ = spectra[:, :LANES], spectra[:, LANES:]
        hr_, hi_ = hspec[g, :, :LANES], hspec[g, :, LANES:]
        product = jnp.concatenate([xr_ * hr_ - xi_ * hi_, xr_ * hi_ + xi_ * hr_], axis=1)
        back = dot3(product, back_t)
        cosine, sine = turn_t[0], turn_t[1]
        sums = []
        for j in range(group):
            real = back[j * padded:(j + 1) * padded, :LANES]
            imag = back[j * padded:(j + 1) * padded, LANES:]
            sums.append(jnp.concatenate([real * cosine + imag * sine, imag * cosine - real * sine], axis=0))
        high, low = split(jnp.concatenate(sums, axis=1))
        conv = dot(close_t[0], high) + (dot(close_t[0], low) + dot(close_t[1], high))
        for j in range(group):
            y32[:, j * blocks:(j + 1) * blocks, :] = conv[:, j * LANES:(j + 1) * LANES].reshape(shards, blocks, LANES)
        ys[g] = y32[...].astype(BF16)
        y_swap("start", g)
        yr[g, seq] = ys[g, seq]

    def gated_copy(g, slot, peer, owner):
        return remote(gbuf.at[chan, g], gbuf.at[owner, g], g_send.at[slot, g], g_recv.at[owner, g], (seq, peer))

    def gated_fwd(g, owner):
        return remote(gbuf.at[owner, g], gbuf.at[owner, g], gf_send.at[g], g_recv.at[owner, g], (seq, core_peer))

    def gate(g):
        y_swap("recv", g)
        c32[...] = yr[g].reshape(c32.shape).astype(F32)
        for block in range(blocks):
            pieces = []
            for c in range(group):
                conv = c32[pl.ds(c * blocks + block, shards, stride=group * blocks), :]
                at = pl.ds(block * LANES + g * group + c, shards, stride=cd)
                pieces.append(keep_t[at, :] * (conv + skip_t[at, :]))
            gbuf[chan, g, :, block * LANES:(block + 1) * LANES] = jnp.concatenate(pieces, axis=0).astype(BF16)
        gated_copy(g, 1, x_peer, chan).start()
        gated_copy(g, 0, core_peer, chan).start()

    def forward(g):
        gated_copy(g, 1, x_peer, x_peer).wait_recv()
        gated_fwd(g, x_peer).start()

    def mix(g):
        gated_copy(g, 0, core_peer, core_peer).wait_recv()
        gated_copy(g, 0, core_peer, diag).wait_recv()
        whole = jnp.concatenate([gbuf[j, g] for j in range(chans)], axis=0)
        weights = jnp.concatenate([wt[g, j] for j in range(chans)], axis=0)
        part = dot(weights.astype(F32).T.astype(BF16), whole)
        if g > 0:
            part = part + acc[...]
        if g < groups - 1:
            acc[...] = part
        else:
            for block in range(blocks):
                span = slice(block * LANES, (block + 1) * LANES)
                out[span, :] = part[:, span].T.astype(BF16)

    for g in range(groups):
        convolve(g)
        if g >= 1:
            gate(g - 1)
        if g >= 2:
            forward(g - 2)
    gate(groups - 1)
    for g in range(max(groups - 2, 0), groups - 1):
        forward(g)
    for g in range(groups - 2):
        mix(g)
    forward(groups - 1)
    for g in range(max(groups - 2, 0), groups):
        mix(g)

    for k in range(chunks + 1):
        tok_copy(k, 1, x_peer, chan).wait_send()
        tok_copy(k, 0, core_peer, chan).wait_send()
        fwd_copy(k, x_peer).wait_send()
    for slot, peer in enumerate(others):
        wo_copy(slot, peer, chan).wait_send()
    rim_copy().wait_send()
    for half in range(2):
        h_swap("send", half)
    for part in range(parts):
        x_swap("send", part)
    for g in range(groups):
        y_swap("send", g)
        gated_copy(g, 1, x_peer, chan).wait_send()
        gated_copy(g, 0, core_peer, chan).wait_send()
        gated_fwd(g, x_peer).wait_send()


def on_device(shards, chans, tokens, w_in, short_filter, long_filter, skip_gain, w_out):
    count, width = tokens.shape
    length = shards * count
    blocks = count // LANES
    cd = width // shards
    chunks = 4
    parts = 4 if blocks // 4 * cd % 16 == 0 else 2
    group = min(cd, 4)
    groups = cd // group
    consts = tables(2 * length)
    outer, turn, ahead, back, close = consts
    wide = 3 * width
    inputs = w_in.shape[0]
    dma = pltpu.SemaphoreType.DMA
    vmem = pltpu.VMEM
    swap_shape = (shards, blocks * cd, LANES)
    flat_shape = (shards * blocks * cd, LANES)
    back_shape = (groups, shards, group * blocks, LANES)
    operands = (
        tokens, w_in.transpose(1, 0, 2), short_filter, long_filter,
        skip_gain.reshape(1, width), w_out,
    ) + tuple(jnp.asarray(c) for c in consts)
    return pl.pallas_call(
        functools.partial(kernel, shards, chans, chunks, parts, group),
        out_shape=jax.ShapeDtypeStruct((count, width), BF16),
        in_specs=[pl.BlockSpec(memory_space=pl.ANY)] * len(operands),
        out_specs=pl.BlockSpec(memory_space=vmem),
        scratch_shapes=[
            vmem((chans, count, width), BF16),
            vmem((chans, RIM, width), BF16),
            vmem((inputs, wide), BF16),
            vmem(short_filter.shape, F32),
            vmem((count, width), F32),
            vmem((1, width), F32),
        ] + [vmem(c.shape, F32) for c in consts] + [
            vmem(outer.shape, BF16),
            vmem((2,) + ahead.shape, BF16),
            vmem((2,) + back.shape, BF16),
            vmem((2,) + close.shape, BF16),
            vmem((RIM + count, wide), F32),
            vmem((RIM, wide), BF16),
            vmem((RIM, wide), BF16),
            vmem((count, width), F32),
            vmem((blocks * LANES, LANES), F32),
            vmem((blocks * LANES, LANES), F32),
            vmem(swap_shape, F32),
            vmem(swap_shape, BF16),
            vmem(swap_shape, BF16),
            vmem(swap_shape, BF16),
            vmem(swap_shape, BF16),
            vmem(back_shape, BF16),
            vmem(back_shape, BF16),
            vmem(flat_shape, F32),
            vmem(flat_shape, F32),
            vmem((groups, group * turn.shape[1], 2 * LANES), F32),
            vmem(back_shape[1:], F32),
            vmem((shards * group * blocks, LANES), F32),
            vmem((chans, groups, group * shards, count), BF16),
            vmem((chans, width, LANES), BF16),
            vmem((width, LANES), F32),
            vmem((groups, chans, group * shards, LANES), BF16),
            vmem((LANES, count), F32),
            dma((14,)),
            dma((2, chunks + 1)), dma((chans, chunks + 1)), dma((chunks + 1,)),
            dma((3,)), dma((chans,)), dma, dma,
            dma((2, shards)), dma((2, shards)),
            dma((parts, shards)), dma((parts, shards)),
            dma((groups, shards)), dma((groups, shards)),
            dma((2, groups)), dma((chans, groups)), dma((groups,)),
        ],
        compiler_params=pltpu.CompilerParams(
            collective_id=0, has_side_effects=True, vmem_limit_bytes=56 * 1024 * 1024
        ),
        cost_estimate=pl.CostEstimate(flops=4 * 10**9, bytes_accessed=4 * 10**6, transcendentals=0),
    )(*operands)


def solution(mesh):
    shards, chans = mesh.shape["seq"], mesh.shape["chan"]
    return jax.shard_map(
        functools.partial(on_device, shards, chans),
        mesh=mesh,
        in_specs=(
            P("seq", "chan"),
            P(None, None, "chan"),
            P(None, None, "chan"),
            P("seq", "chan"),
            P("chan"),
            P("chan", None),
        ),
        out_specs=P("seq", "chan"),
        check_vma=False,
    )
```

```python
import functools
import math

import jax
import jax.numpy as jnp
import numpy as np
from jax import lax
from jax.experimental import pallas as pl
from jax.experimental.pallas import tpu as pltpu
from jax.sharding import PartitionSpec as P

MESH = pl.DeviceIdType.MESH
LANES = 128
RIM = 16
F32 = jnp.float32
BF16 = jnp.bfloat16


def split(values):
    high = values.astype(BF16)
    low = (values - high.astype(F32)).astype(BF16)
    return high, low


def split_table(table):
    table = np.asarray(table, np.float64)
    high = table.astype(np.float32).astype(BF16)
    low = (table - high.astype(np.float64)).astype(np.float32).astype(BF16)
    return high, low


def tables(total):
    first = total // LANES
    half = first // 2
    kept = half + 1
    padded = -(-kept // 16) * 16
    k1 = np.arange(padded)
    live = (k1 < kept).astype(np.float64)[:, None]
    n1 = np.arange(half)
    angle = 2.0 * math.pi / first * (k1[:, None] * n1[None, :] % first)
    outer = np.concatenate([np.cos(angle) * live, -np.sin(angle) * live], axis=0)
    outer_table = np.concatenate(split_table(outer), axis=1).astype(np.float32)
    n2 = np.arange(LANES)
    turn = 2.0 * math.pi / total * (k1[:, None] * n2[None, :] % total)
    turn_table = np.stack([np.cos(turn), -np.sin(turn)]).astype(np.float32)
    inner = 2.0 * math.pi / LANES * (n2[:, None] * n2[None, :] % LANES)
    cosine, sine = np.cos(inner), -np.sin(inner)
    ahead = np.block([[cosine, sine], [-sine, cosine]])
    ahead_table = ahead.astype(np.float32)
    back_table = ahead.T.astype(np.float32)
    weight = np.where((k1 == 0) | (k1 == half), 1.0, 2.0) * live[:, 0] / total
    close = np.concatenate([np.cos(angle).T * weight, -np.sin(angle).T * weight], axis=1)
    close_table = close.astype(np.float32)
    return outer_table, turn_table, ahead_table, back_table, close_table


def dot(left, right):
    return jnp.dot(left, right, preferred_element_type=F32)


def dot2(left, table_ref):
    rounded = left.astype(BF16)
    return dot(rounded, table_ref[0]) + dot(rounded, table_ref[1])


def kernel(
    shards, chans, chunks, parts, group,
    tok, w_in, sfilt_a, lfilt_a, gain_a, w_out, outer_a, turn_a, ahead_a, back_a, close_a,
    out,
    tbuf, tmini, w, sfilt, lfilt, gain, outer_f, turn_t, ahead_f, back_f, close_f,
    outer_t, ahead_t, back_t, close_t,
    proj, rim_out, rim_in, keep, keep_t, skip_t, stage, hs, hr, xs, xr, ys, yr,
    x32, h32, hspec, y32, c32, gbuf, wbuf, w32, w_rows, wt, acc, gain_rows,
    local, tok_send, tok_recv, fwd_send, wo_send, wo_recv, rim_send, rim_recv,
    h_send, h_recv, x_send, x_recv, y_send, y_recv, g_send, g_recv, gf_send,
):
    seq = lax.axis_index("seq")
    chan = lax.axis_index("chan")
    count = tok.shape[0]
    blocks = count // LANES
    cd = LANES // shards
    groups = cd // group
    rows = count // chunks
    core_peer = chan + 1 - 2 * (chan % 2)
    x_peer = (chan + 2) % chans
    diag = (core_peer + 2) % chans
    others = (core_peer, x_peer, diag)
    far_first = sorted(range(1, shards), key=lambda d: -min(d, shards - d))

    own_columns = pl.ds(pl.multiple_of(chan * LANES, LANES), LANES)
    loads = [(lfilt_a, lfilt), (tok, tbuf.at[chan]), (tok.at[pl.ds(count - RIM, RIM)], tmini.at[chan])]
    loads += [(w_in.at[g], w.at[:, pl.ds(g * LANES, LANES)]) for g in range(3)]
    loads += [(sfilt_a, sfilt), (gain_a, gain), (w_out.at[:, own_columns], wbuf.at[chan])]
    loads += [(outer_a, outer_f), (turn_a, turn_t), (ahead_a, ahead_f), (back_a, back_f), (close_a, close_f)]
    copies = [pltpu.make_async_copy(src, dst, local.at[i]) for i, (src, dst) in enumerate(loads)]
    for copy in copies:
        copy.start()

    barrier = pltpu.get_barrier_semaphore()
    for peer in others:
        pl.semaphore_signal(barrier, inc=1, device_id=(seq, peer), device_id_type=MESH)

    def greet(d, carry):
        peer = (seq + d) % shards
        pl.semaphore_signal(barrier, inc=1, device_id=(peer, chan), device_id_type=MESH)
        return carry

    lax.fori_loop(1, shards, greet, 0)

    def spread(turned, block):
        for dest in range(shards):
            stage[dest, block * cd:(block + 1) * cd, :] = turned[dest * cd:(dest + 1) * cd, :]

    def pack(dst, part, pieces):
        size = blocks // pieces * cd
        span = slice(part * size, (part + 1) * size)
        dst[:, span, :] = stage[:, span, :].astype(BF16)

    copies[0].wait()
    for block in range(blocks):
        spread(lfilt[block * LANES:(block + 1) * LANES, :].T, block)
    pack(hs, 0, 1)
    for copy in copies[1:]:
        copy.wait()
    gain_rows[...] = jnp.broadcast_to(gain[...], (LANES, LANES)).T
    outer_t[...] = outer_f[...].astype(BF16)
    for table, ref in ((ahead_f, ahead_t), (back_f, back_t), (close_f, close_t)):
        high, low = split(table[...])
        ref[0] = high
        ref[1] = low
    pl.semaphore_wait(barrier, len(others) + shards - 1)

    def remote(src, dst, send, recv, device):
        return pltpu.make_async_remote_copy(
            src_ref=src, dst_ref=dst, send_sem=send, recv_sem=recv,
            device_id=device, device_id_type=MESH,
        )

    def landing(k, owner):
        if k == 0:
            return tmini.at[owner]
        return tbuf.at[owner, pl.ds((k - 1) * rows, rows)]

    def tok_copy(k, slot, peer, owner):
        span = pl.ds(count - RIM, RIM) if k == 0 else pl.ds((k - 1) * rows, rows)
        return remote(tok.at[span], landing(k, owner), tok_send.at[slot, k], tok_recv.at[owner, k], (seq, peer))

    def fwd_copy(k, owner):
        return remote(landing(k, owner), landing(k, owner), fwd_send.at[k], tok_recv.at[owner, k], (seq, core_peer))

    for k in range(chunks + 1):
        tok_copy(k, 1, x_peer, chan).start()
        tok_copy(k, 0, core_peer, chan).start()

    def wo_copy(slot, peer, owner):
        columns = pl.ds(pl.multiple_of(peer * LANES, LANES), LANES)
        return remote(w_out.at[:, columns], wbuf.at[owner], wo_send.at[slot], wo_recv.at[owner], (seq, peer))

    def swap_all(action, src, dst, send, recv, part, span):
        if action == "start":
            for d in far_first:
                peer = (seq + d) % shards
                remote(src.at[peer, span], dst.at[seq, span], send.at[part], recv.at[part], (peer, chan)).start()
            return
        several = pl.ds(0, shards - 1)
        whole = remote(
            src.at[several, span], dst.at[several, span], send.at[part], recv.at[part], ((seq + 1) % shards, chan)
        )
        if action == "recv":
            whole.wait_recv()
        else:
            whole.wait_send()

    def h_swap(action, half):
        size = blocks // 2 * cd
        swap_all(action, hs, hr, h_send, h_recv, half, pl.ds(half * size, size))

    def x_swap(action, part):
        size = blocks // parts * cd
        swap_all(action, xs, xr, x_send, x_recv, part, pl.ds(part * size, size))

    def y_swap(action, g):
        swap_all(action, ys.at[g], yr.at[g], y_send, y_recv, g, pl.ds(0, group * blocks))

    for half in range(2):
        h_swap("start", half)
    hr[seq] = hs[seq]
    for slot, peer in enumerate(others):
        wo_copy(slot, peer, chan).start()

    def shorten(k):
        for g in range(3):
            lanes = slice(g * LANES, (g + 1) * LANES)
            base = RIM + k * rows
            value = (
                sfilt[0, g:g + 1, :] * proj[base:base + rows, lanes]
                + sfilt[1, g:g + 1, :] * proj[base - 1:base - 1 + rows, lanes]
                + sfilt[2, g:g + 1, :] * proj[base - 2:base - 2 + rows, lanes]
            )
            if g == 0:
                held = value
            elif g == 1:
                held = held * value
            else:
                keep[k * rows:(k + 1) * rows, :] = value
        for j in range(rows // LANES):
            block = k * (rows // LANES) + j
            turned = held[j * LANES:(j + 1) * LANES, :].T
            spread(turned, block)
            skip_t[block * LANES:(block + 1) * LANES, :] = turned * gain_rows[...]

    def rim_copy():
        return remote(rim_out, rim_in, rim_send, rim_recv, ((seq + 1) % shards, chan))

    def take(k):
        tok_copy(k, 1, x_peer, x_peer).wait_recv()
        fwd_copy(k, x_peer).start()
        tok_copy(k, 0, core_peer, core_peer).wait_recv()
        tok_copy(k, 0, core_peer, diag).wait_recv()

    take(0)
    tail = jnp.concatenate([tmini[j] for j in range(chans)], axis=1)
    rim_out[...] = dot(tail, w[...]).astype(BF16)
    rim_copy().start()
    for k in range(chunks):
        take(k + 1)
        features = jnp.concatenate([tbuf[j, k * rows:(k + 1) * rows, :] for j in range(chans)], axis=1)
        projected = dot(features, w[...]).astype(BF16)
        proj[RIM + k * rows:RIM + (k + 1) * rows, :] = projected.astype(F32)
        if k == 0:
            rim_copy().wait_recv()
            live = (seq > 0).astype(F32)
            proj[0:RIM, :] = rim_in[...].astype(F32) * live
        shorten(k)
        if (k + 1) * parts % chunks == 0:
            part = (k + 1) * parts // chunks - 1
            pack(xs, part, parts)
            x_swap("start", part)
    xr[seq] = xs[seq]

    height = shards * blocks
    padded = turn_t.shape[1]
    edge = group * padded

    def spectrum(ref, g, product):
        columns = [ref[pl.ds(g * group + j, height, stride=cd), :].astype(BF16) for j in range(group)]
        signal = jnp.concatenate(columns, axis=1)
        signal = jnp.concatenate([signal, signal], axis=0)
        opened = dot(outer_t[...], signal)
        cosine, sine = turn_t[0], turn_t[1]
        turned = []
        for j in range(group):
            real = opened[:padded, j * LANES:(j + 1) * LANES]
            imag = opened[padded:, j * LANES:(j + 1) * LANES]
            turned.append(jnp.concatenate([real * cosine - imag * sine, real * sine + imag * cosine], axis=1))
        return product(jnp.concatenate(turned, axis=0), ahead_t)

    def dot1(left, table_ref):
        return dot(left.astype(BF16), table_ref[0])

    for half in range(2):
        h_swap("recv", half)
    h32[...] = hr[...].reshape(h32.shape).astype(F32)
    for g in range(groups):
        hspec[g] = spectrum(h32, g, dot2)
    for block in range(blocks):
        span = slice(block * LANES, (block + 1) * LANES)
        keep_t[span, :] = keep[span, :].T
    for slot, peer in enumerate(others):
        wo_copy(slot, peer, peer).wait_recv()
    for j in range(chans):
        w32[...] = wbuf[j].astype(F32)
        for g in range(groups):
            picked = [w32[pl.ds(g * group + c, shards, stride=cd), :] for c in range(group)]
            w_rows[g, j] = jnp.concatenate(picked, axis=0)
    for g in range(groups):
        wt[g] = jnp.concatenate([w_rows[g, j] for j in range(chans)], axis=0).T.astype(BF16)

    for k in range(chunks + 1):
        tok_copy(k, 1, x_peer, chan).wait_send()
        tok_copy(k, 0, core_peer, chan).wait_send()
        fwd_copy(k, x_peer).wait_send()
    for slot, peer in enumerate(others):
        wo_copy(slot, peer, chan).wait_send()
    rim_copy().wait_send()
    for half in range(2):
        h_swap("send", half)

    for part in range(parts):
        x_swap("recv", part)
    x32[...] = xr[...].reshape(x32.shape).astype(F32)

    def convolve(g):
        spectra = spectrum(x32, g, dot1)
        xr_, xi_ = spectra[:, :LANES], spectra[:, LANES:]
        hr_, hi_ = hspec[g, :, :LANES], hspec[g, :, LANES:]
        product = jnp.concatenate([xr_ * hr_ - xi_ * hi_, xr_ * hi_ + xi_ * hr_], axis=1)
        back = dot1(product, back_t)
        cosine, sine = turn_t[0], turn_t[1]
        sums = []
        for j in range(group):
            real = back[j * padded:(j + 1) * padded, :LANES]
            imag = back[j * padded:(j + 1) * padded, LANES:]
            sums.append(jnp.concatenate([real * cosine + imag * sine, imag * cosine - real * sine], axis=0))
        conv = dot(close_t[0], jnp.concatenate(sums, axis=1).astype(BF16))
        for j in range(group):
            y32[:, j * blocks:(j + 1) * blocks, :] = conv[:, j * LANES:(j + 1) * LANES].reshape(shards, blocks, LANES)
        ys[g] = y32[...].astype(BF16)
        y_swap("start", g)
        yr[g, seq] = ys[g, seq]

    def gated_copy(g, slot, peer, owner):
        return remote(gbuf.at[chan, g], gbuf.at[owner, g], g_send.at[slot, g], g_recv.at[owner, g], (seq, peer))

    def gated_fwd(g, owner):
        return remote(gbuf.at[owner, g], gbuf.at[owner, g], gf_send.at[g], g_recv.at[owner, g], (seq, core_peer))

    def gate(g):
        y_swap("recv", g)
        c32[...] = yr[g].reshape(c32.shape).astype(F32)
        for block in range(blocks):
            pieces = []
            for c in range(group):
                conv = c32[pl.ds(c * blocks + block, shards, stride=group * blocks), :]
                at = pl.ds(block * LANES + g * group + c, shards, stride=cd)
                pieces.append(keep_t[at, :] * (conv + skip_t[at, :]))
            gbuf[chan, g, :, block * LANES:(block + 1) * LANES] = jnp.concatenate(pieces, axis=0).astype(BF16)
        gated_copy(g, 1, x_peer, chan).start()
        gated_copy(g, 0, core_peer, chan).start()

    def forward(g):
        gated_copy(g, 1, x_peer, x_peer).wait_recv()
        gated_fwd(g, x_peer).start()

    def mix(g):
        gated_copy(g, 0, core_peer, core_peer).wait_recv()
        gated_copy(g, 0, core_peer, diag).wait_recv()
        whole = jnp.concatenate([gbuf[j, g] for j in range(chans)], axis=0)
        part = dot(wt[g], whole)
        if g > 0:
            part = part + acc[...]
        if g < groups - 1:
            acc[...] = part
        else:
            for block in range(blocks):
                span = slice(block * LANES, (block + 1) * LANES)
                out[span, :] = part[:, span].T.astype(BF16)

    for g in range(groups):
        convolve(g)
        if g >= 1:
            gate(g - 1)
        if g >= 2:
            forward(g - 2)
    for part in range(parts):
        x_swap("send", part)
    gate(groups - 1)
    for g in range(groups):
        y_swap("send", g)
    for g in range(max(groups - 2, 0), groups - 1):
        forward(g)
    for g in range(groups - 2):
        mix(g)
    forward(groups - 1)
    for g in range(max(groups - 2, 0), groups):
        mix(g)

    for g in range(groups):
        gated_copy(g, 1, x_peer, chan).wait_send()
        gated_copy(g, 0, core_peer, chan).wait_send()
        gated_fwd(g, x_peer).wait_send()


def on_device(shards, chans, tokens, w_in, short_filter, long_filter, skip_gain, w_out):
    count, width = tokens.shape
    length = shards * count
    blocks = count // LANES
    cd = width // shards
    chunks = 4
    parts = 4 if blocks // 4 * cd % 16 == 0 else 2
    group = min(cd, 4)
    groups = cd // group
    consts = tables(2 * length)
    outer, turn, ahead, back, close = consts
    wide = 3 * width
    inputs = w_in.shape[0]
    dma = pltpu.SemaphoreType.DMA
    vmem = pltpu.VMEM
    swap_shape = (shards, blocks * cd, LANES)
    flat_shape = (shards * blocks * cd, LANES)
    back_shape = (groups, shards, group * blocks, LANES)
    operands = (
        tokens, w_in.transpose(1, 0, 2), short_filter, long_filter,
        skip_gain.reshape(1, width), w_out,
    ) + tuple(jnp.asarray(c) for c in consts)
    return pl.pallas_call(
        functools.partial(kernel, shards, chans, chunks, parts, group),
        out_shape=jax.ShapeDtypeStruct((count, width), BF16),
        in_specs=[pl.BlockSpec(memory_space=pl.ANY)] * len(operands),
        out_specs=pl.BlockSpec(memory_space=vmem),
        scratch_shapes=[
            vmem((chans, count, width), BF16),
            vmem((chans, RIM, width), BF16),
            vmem((inputs, wide), BF16),
            vmem(short_filter.shape, F32),
            vmem((count, width), F32),
            vmem((1, width), F32),
        ] + [vmem(c.shape, F32) for c in consts] + [
            vmem(outer.shape, BF16),
            vmem((2,) + ahead.shape, BF16),
            vmem((2,) + back.shape, BF16),
            vmem((2,) + close.shape, BF16),
            vmem((RIM + count, wide), F32),
            vmem((RIM, wide), BF16),
            vmem((RIM, wide), BF16),
            vmem((count, width), F32),
            vmem((blocks * LANES, LANES), F32),
            vmem((blocks * LANES, LANES), F32),
            vmem(swap_shape, F32),
            vmem(swap_shape, BF16),
            vmem(swap_shape, BF16),
            vmem(swap_shape, BF16),
            vmem(swap_shape, BF16),
            vmem(back_shape, BF16),
            vmem(back_shape, BF16),
            vmem(flat_shape, F32),
            vmem(flat_shape, F32),
            vmem((groups, group * turn.shape[1], 2 * LANES), F32),
            vmem(back_shape[1:], F32),
            vmem((shards * group * blocks, LANES), F32),
            vmem((chans, groups, group * shards, count), BF16),
            vmem((chans, width, LANES), BF16),
            vmem((width, LANES), F32),
            vmem((groups, chans, group * shards, LANES), F32),
            vmem((groups, LANES, chans * group * shards), BF16),
            vmem((LANES, count), F32),
            vmem((LANES, LANES), F32),
            dma((14,)),
            dma((2, chunks + 1)), dma((chans, chunks + 1)), dma((chunks + 1,)),
            dma((3,)), dma((chans,)), dma, dma,
            dma((2,)), dma((2,)),
            dma((parts,)), dma((parts,)),
            dma((groups,)), dma((groups,)),
            dma((2, groups)), dma((chans, groups)), dma((groups,)),
        ],
        compiler_params=pltpu.CompilerParams(
            collective_id=0, has_side_effects=True, vmem_limit_bytes=56 * 1024 * 1024
        ),
        cost_estimate=pl.CostEstimate(flops=4 * 10**9, bytes_accessed=4 * 10**6, transcendentals=0),
    )(*operands)


def solution(mesh):
    shards, chans = mesh.shape["seq"], mesh.shape["chan"]
    return jax.shard_map(
        functools.partial(on_device, shards, chans),
        mesh=mesh,
        in_specs=(
            P("seq", "chan"),
            P(None, None, "chan"),
            P(None, None, "chan"),
            P("seq", "chan"),
            P("chan"),
            P("chan", None),
        ),
        out_specs=P("seq", "chan"),
        check_vma=False,
    )
```

```python
import functools
import math

import jax
import jax.numpy as jnp
import numpy as np
from jax import lax
from jax.experimental import pallas as pl
from jax.experimental.pallas import tpu as pltpu
from jax.sharding import PartitionSpec as P

MESH = pl.DeviceIdType.MESH
LANES = 128
RIM = 16
F32 = jnp.float32
BF16 = jnp.bfloat16


def split(values):
    high = values.astype(BF16)
    low = (values - high.astype(F32)).astype(BF16)
    return high, low


def split_table(table):
    table = np.asarray(table, np.float64)
    high = table.astype(np.float32).astype(BF16)
    low = (table - high.astype(np.float64)).astype(np.float32).astype(BF16)
    return high, low


def tables(total):
    first = total // LANES
    half = first // 2
    kept = half + 1
    padded = -(-kept // 16) * 16
    k1 = np.arange(padded)
    live = (k1 < kept).astype(np.float64)[:, None]
    n1 = np.arange(half)
    angle = 2.0 * math.pi / first * (k1[:, None] * n1[None, :] % first)
    outer = np.concatenate([np.cos(angle) * live, -np.sin(angle) * live], axis=0)
    outer_table = np.concatenate(split_table(outer), axis=1).astype(np.float32)
    n2 = np.arange(LANES)
    turn = 2.0 * math.pi / total * (k1[:, None] * n2[None, :] % total)
    turn_table = np.stack([np.cos(turn), -np.sin(turn)]).astype(np.float32)
    inner = 2.0 * math.pi / LANES * (n2[:, None] * n2[None, :] % LANES)
    cosine, sine = np.cos(inner), -np.sin(inner)
    ahead = np.block([[cosine, sine], [-sine, cosine]])
    ahead_table = ahead.astype(np.float32)
    back_table = ahead.T.astype(np.float32)
    weight = np.where((k1 == 0) | (k1 == half), 1.0, 2.0) * live[:, 0] / total
    close = np.concatenate([np.cos(angle).T * weight, -np.sin(angle).T * weight], axis=1)
    close_table = close.astype(np.float32)
    return outer_table, turn_table, ahead_table, back_table, close_table


def dot(left, right):
    return jnp.dot(left, right, preferred_element_type=F32)


def each(low, high, body):
    def one(i, carry):
        body(i)
        return carry

    lax.fori_loop(low, high, one, 0)


def piece(start, size):
    return pl.ds(pl.multiple_of(start, size), size)


def dot2(left, table_ref):
    rounded = left.astype(BF16)
    return dot(rounded, table_ref[0]) + dot(rounded, table_ref[1])


def kernel(
    shards, chans, chunks, parts, group,
    tok, w_in, sfilt_a, lfilt_a, gain_a, w_out, outer_a, turn_a, ahead_a, back_a, close_a,
    out,
    tbuf, tmini, w, sfilt, lfilt, gain, outer_f, turn_t, ahead_f, back_f, close_f,
    outer_t, ahead_t, back_t, close_t,
    proj, rim_out, rim_in, keep, keep_t, skip_t, stage, hs, hr, xs, xr, ys, yr,
    x32, h32, hspec, y32, c32, gbuf, wbuf, w32, w_rows, wt, acc, gain_rows,
    local, tok_send, tok_recv, fwd_send, wo_send, wo_recv, rim_send, rim_recv,
    h_send, h_recv, x_send, x_recv, y_send, y_recv, g_send, g_recv, gf_send,
):
    seq = lax.axis_index("seq")
    chan = lax.axis_index("chan")
    count = tok.shape[0]
    blocks = count // LANES
    cd = LANES // shards
    groups = cd // group
    rows = count // chunks
    core_peer = chan + 1 - 2 * (chan % 2)
    x_peer = (chan + 2) % chans
    diag = (core_peer + 2) % chans
    others = (core_peer, x_peer, diag)
    far_first = sorted(range(1, shards), key=lambda d: -min(d, shards - d))

    own_columns = pl.ds(pl.multiple_of(chan * LANES, LANES), LANES)
    loads = [(lfilt_a, lfilt), (tok, tbuf.at[chan]), (tok.at[pl.ds(count - RIM, RIM)], tmini.at[chan])]
    loads += [(w_in.at[g], w.at[:, pl.ds(g * LANES, LANES)]) for g in range(3)]
    loads += [(sfilt_a, sfilt), (gain_a, gain), (w_out.at[:, own_columns], wbuf.at[chan])]
    loads += [(outer_a, outer_f), (turn_a, turn_t), (ahead_a, ahead_f), (back_a, back_f), (close_a, close_f)]
    copies = [pltpu.make_async_copy(src, dst, local.at[i]) for i, (src, dst) in enumerate(loads)]
    for copy in copies:
        copy.start()

    barrier = pltpu.get_barrier_semaphore()
    for peer in others:
        pl.semaphore_signal(barrier, inc=1, device_id=(seq, peer), device_id_type=MESH)

    @functools.partial(each, 1, shards)
    def greet(d):
        peer = (seq + d) % shards
        pl.semaphore_signal(barrier, inc=1, device_id=(peer, chan), device_id_type=MESH)

    def spread(turned, block):
        for dest in range(shards):
            stage[dest, piece(block * cd, cd), :] = turned[dest * cd:(dest + 1) * cd, :]

    def pack(dst, part, pieces):
        size = blocks // pieces * cd
        span = piece(part * size, size)
        dst[:, span, :] = stage[:, span, :].astype(BF16)

    copies[0].wait()
    each(0, blocks, lambda block: spread(lfilt[piece(block * LANES, LANES), :].T, block))
    pack(hs, 0, 1)
    for copy in copies[1:]:
        copy.wait()
    gain_rows[...] = jnp.broadcast_to(gain[...], (LANES, LANES)).T
    outer_t[...] = outer_f[...].astype(BF16)
    for table, ref in ((ahead_f, ahead_t), (back_f, back_t), (close_f, close_t)):
        high, low = split(table[...])
        ref[0] = high
        ref[1] = low
    pl.semaphore_wait(barrier, len(others) + shards - 1)

    def remote(src, dst, send, recv, device):
        return pltpu.make_async_remote_copy(
            src_ref=src, dst_ref=dst, send_sem=send, recv_sem=recv,
            device_id=device, device_id_type=MESH,
        )

    def first(k):
        return isinstance(k, int) and k == 0

    def landing(k, owner):
        if first(k):
            return tmini.at[owner]
        return tbuf.at[owner, piece((k - 1) * rows, rows)]

    def tok_copy(k, slot, peer, owner):
        span = pl.ds(count - RIM, RIM) if first(k) else piece((k - 1) * rows, rows)
        return remote(tok.at[span], landing(k, owner), tok_send.at[slot, k], tok_recv.at[owner, k], (seq, peer))

    def fwd_copy(k, owner):
        return remote(landing(k, owner), landing(k, owner), fwd_send.at[k], tok_recv.at[owner, k], (seq, core_peer))

    def give(k):
        tok_copy(k, 1, x_peer, chan).start()
        tok_copy(k, 0, core_peer, chan).start()

    give(0)
    each(1, chunks + 1, give)

    def wo_copy(slot, peer, owner):
        columns = pl.ds(pl.multiple_of(peer * LANES, LANES), LANES)
        return remote(w_out.at[:, columns], wbuf.at[owner], wo_send.at[slot], wo_recv.at[owner], (seq, peer))

    def swap_all(action, src, dst, send, recv, part, span):
        if action == "start":
            for d in far_first:
                peer = (seq + d) % shards
                remote(src.at[peer, span], dst.at[seq, span], send.at[part], recv.at[part], (peer, chan)).start()
            return
        several = pl.ds(0, shards - 1)
        whole = remote(
            src.at[several, span], dst.at[several, span], send.at[part], recv.at[part], ((seq + 1) % shards, chan)
        )
        if action == "recv":
            whole.wait_recv()
        else:
            whole.wait_send()

    def h_swap(action, half):
        size = blocks // 2 * cd
        swap_all(action, hs, hr, h_send, h_recv, half, pl.ds(half * size, size))

    def x_swap(action, part):
        size = blocks // parts * cd
        swap_all(action, xs, xr, x_send, x_recv, part, piece(part * size, size))

    def y_swap(action, g):
        swap_all(action, ys.at[g], yr.at[g], y_send, y_recv, g, pl.ds(0, group * blocks))

    for half in range(2):
        h_swap("start", half)
    hr[seq] = hs[seq]
    for slot, peer in enumerate(others):
        wo_copy(slot, peer, chan).start()

    def shorten(k):
        for g in range(3):
            lanes = slice(g * LANES, (g + 1) * LANES)
            base = pl.multiple_of(RIM // 2 + k * rows, 8)
            window = proj[pl.ds(base, rows + 8), lanes]
            value = (
                sfilt[0, g:g + 1, :] * window[8:, :]
                + sfilt[1, g:g + 1, :] * window[7:-1, :]
                + sfilt[2, g:g + 1, :] * window[6:-2, :]
            )
            if g == 0:
                held = value
            elif g == 1:
                held = held * value
            else:
                keep[piece(k * rows, rows), :] = value
        for j in range(rows // LANES):
            block = k * (rows // LANES) + j
            turned = held[j * LANES:(j + 1) * LANES, :].T
            spread(turned, block)
            skip_t[piece(block * LANES, LANES), :] = turned * gain_rows[...]

    def rim_copy():
        return remote(rim_out, rim_in, rim_send, rim_recv, ((seq + 1) % shards, chan))

    def take(k):
        tok_copy(k, 1, x_peer, x_peer).wait_recv()
        fwd_copy(k, x_peer).start()
        tok_copy(k, 0, core_peer, core_peer).wait_recv()
        tok_copy(k, 0, core_peer, diag).wait_recv()

    take(0)
    tail = jnp.concatenate([tmini[j] for j in range(chans)], axis=1)
    rim_out[...] = dot(tail, w[...]).astype(BF16)
    rim_copy().start()
    @functools.partial(each, 0, parts)
    def project(part):
        for i in range(chunks // parts):
            k = part * (chunks // parts) + i
            take(k + 1)
            span = piece(k * rows, rows)
            features = jnp.concatenate([tbuf[j, span, :] for j in range(chans)], axis=1)
            projected = dot(features, w[...]).astype(BF16)
            proj[pl.ds(pl.multiple_of(RIM + k * rows, RIM), rows), :] = projected.astype(F32)
            if i == 0:
                @pl.when(part == 0)
                def edge_rows():
                    rim_copy().wait_recv()
                    live = (seq > 0).astype(F32)
                    proj[0:RIM, :] = rim_in[...].astype(F32) * live
            shorten(k)
        pack(xs, part, parts)
        x_swap("start", part)

    xr[seq] = xs[seq]

    height = shards * blocks
    padded = turn_t.shape[1]
    edge = group * padded

    def spectrum(ref, g, product):
        columns = [ref[pl.ds(g * group + j, height, stride=cd), :].astype(BF16) for j in range(group)]
        signal = jnp.concatenate(columns, axis=1)
        signal = jnp.concatenate([signal, signal], axis=0)
        opened = dot(outer_t[...], signal)
        cosine, sine = turn_t[0], turn_t[1]
        turned = []
        for j in range(group):
            real = opened[:padded, j * LANES:(j + 1) * LANES]
            imag = opened[padded:, j * LANES:(j + 1) * LANES]
            turned.append(jnp.concatenate([real * cosine - imag * sine, real * sine + imag * cosine], axis=1))
        return product(jnp.concatenate(turned, axis=0), ahead_t)

    def dot1(left, table_ref):
        return dot(left.astype(BF16), table_ref[0])

    for half in range(2):
        h_swap("recv", half)
    h32[...] = hr[...].reshape(h32.shape).astype(F32)

    @functools.partial(each, 0, groups)
    def filter_spectra(g):
        hspec[g] = spectrum(h32, g, dot2)

    @functools.partial(each, 0, blocks)
    def turn_gate(block):
        span = piece(block * LANES, LANES)
        keep_t[span, :] = keep[span, :].T

    for slot, peer in enumerate(others):
        wo_copy(slot, peer, peer).wait_recv()

    @functools.partial(each, 0, chans)
    def turn_weights(j):
        w32[...] = wbuf[j].astype(F32)
        for g in range(groups):
            picked = [w32[pl.ds(g * group + c, shards, stride=cd), :] for c in range(group)]
            w_rows[g, j] = jnp.concatenate(picked, axis=0)

    @functools.partial(each, 0, groups)
    def pack_weights(g):
        wt[g] = jnp.concatenate([w_rows[g, j] for j in range(chans)], axis=0).T.astype(BF16)

    def settle(k):
        tok_copy(k, 1, x_peer, chan).wait_send()
        tok_copy(k, 0, core_peer, chan).wait_send()
        fwd_copy(k, x_peer).wait_send()

    settle(0)
    each(1, chunks + 1, settle)
    acc[...] = jnp.zeros_like(acc)
    for slot, peer in enumerate(others):
        wo_copy(slot, peer, chan).wait_send()
    rim_copy().wait_send()
    for half in range(2):
        h_swap("send", half)

    for part in range(parts):
        x_swap("recv", part)
    x32[...] = xr[...].reshape(x32.shape).astype(F32)

    def convolve(g):
        spectra = spectrum(x32, g, dot1)
        xr_, xi_ = spectra[:, :LANES], spectra[:, LANES:]
        hr_, hi_ = hspec[g, :, :LANES], hspec[g, :, LANES:]
        product = jnp.concatenate([xr_ * hr_ - xi_ * hi_, xr_ * hi_ + xi_ * hr_], axis=1)
        back = dot1(product, back_t)
        cosine, sine = turn_t[0], turn_t[1]
        sums = []
        for j in range(group):
            real = back[j * padded:(j + 1) * padded, :LANES]
            imag = back[j * padded:(j + 1) * padded, LANES:]
            sums.append(jnp.concatenate([real * cosine + imag * sine, imag * cosine - real * sine], axis=0))
        conv = dot(close_t[0], jnp.concatenate(sums, axis=1).astype(BF16))
        for j in range(group):
            y32[:, j * blocks:(j + 1) * blocks, :] = conv[:, j * LANES:(j + 1) * LANES].reshape(shards, blocks, LANES)
        ys[g] = y32[...].astype(BF16)
        y_swap("start", g)
        yr[g, seq] = ys[g, seq]

    def gated_copy(g, slot, peer, owner):
        return remote(gbuf.at[chan, g], gbuf.at[owner, g], g_send.at[slot, g], g_recv.at[owner, g], (seq, peer))

    def gated_fwd(g, owner):
        return remote(gbuf.at[owner, g], gbuf.at[owner, g], gf_send.at[g], g_recv.at[owner, g], (seq, core_peer))

    def gate(g):
        y_swap("recv", g)
        c32[...] = yr[g].reshape(c32.shape).astype(F32)
        for block in range(blocks):
            pieces = []
            for c in range(group):
                conv = c32[pl.ds(c * blocks + block, shards, stride=group * blocks), :]
                at = pl.ds(block * LANES + g * group + c, shards, stride=cd)
                pieces.append(keep_t[at, :] * (conv + skip_t[at, :]))
            gbuf[chan, g, :, block * LANES:(block + 1) * LANES] = jnp.concatenate(pieces, axis=0).astype(BF16)
        gated_copy(g, 1, x_peer, chan).start()
        gated_copy(g, 0, core_peer, chan).start()

    def forward(g):
        gated_copy(g, 1, x_peer, x_peer).wait_recv()
        gated_fwd(g, x_peer).start()

    def mix(g):
        gated_copy(g, 0, core_peer, core_peer).wait_recv()
        gated_copy(g, 0, core_peer, diag).wait_recv()
        whole = jnp.concatenate([gbuf[j, g] for j in range(chans)], axis=0)
        acc[...] += dot(wt[g], whole)

    @functools.partial(each, 0, groups + 1)
    def stream(g):
        pl.when(g < groups)(lambda: convolve(g))
        pl.when(g >= 1)(lambda: gate(g - 1))
        pl.when(g >= 2)(lambda: forward(g - 2))
        pl.when(g >= 3)(lambda: mix(g - 3))

    forward(groups - 1)
    each(0, parts, lambda part: x_swap("send", part))
    each(0, groups, lambda g: y_swap("send", g))
    each(max(groups - 2, 0), groups, mix)
    for block in range(blocks):
        span = slice(block * LANES, (block + 1) * LANES)
        out[span, :] = acc[:, span].T.astype(BF16)

    @functools.partial(each, 0, groups)
    def finish(g):
        gated_copy(g, 1, x_peer, chan).wait_send()
        gated_copy(g, 0, core_peer, chan).wait_send()
        gated_fwd(g, x_peer).wait_send()


def on_device(shards, chans, tokens, w_in, short_filter, long_filter, skip_gain, w_out):
    count, width = tokens.shape
    length = shards * count
    blocks = count // LANES
    cd = width // shards
    chunks = 4
    parts = 4 if blocks // 4 * cd % 16 == 0 else 2
    group = min(cd, 4)
    groups = cd // group
    consts = tables(2 * length)
    outer, turn, ahead, back, close = consts
    wide = 3 * width
    inputs = w_in.shape[0]
    dma = pltpu.SemaphoreType.DMA
    vmem = pltpu.VMEM
    swap_shape = (shards, blocks * cd, LANES)
    flat_shape = (shards * blocks * cd, LANES)
    back_shape = (groups, shards, group * blocks, LANES)
    operands = (
        tokens, w_in.transpose(1, 0, 2), short_filter, long_filter,
        skip_gain.reshape(1, width), w_out,
    ) + tuple(jnp.asarray(c) for c in consts)
    return pl.pallas_call(
        functools.partial(kernel, shards, chans, chunks, parts, group),
        out_shape=jax.ShapeDtypeStruct((count, width), BF16),
        in_specs=[pl.BlockSpec(memory_space=pl.ANY)] * len(operands),
        out_specs=pl.BlockSpec(memory_space=vmem),
        scratch_shapes=[
            vmem((chans, count, width), BF16),
            vmem((chans, RIM, width), BF16),
            vmem((inputs, wide), BF16),
            vmem(short_filter.shape, F32),
            vmem((count, width), F32),
            vmem((1, width), F32),
        ] + [vmem(c.shape, F32) for c in consts] + [
            vmem(outer.shape, BF16),
            vmem((2,) + ahead.shape, BF16),
            vmem((2,) + back.shape, BF16),
            vmem((2,) + close.shape, BF16),
            vmem((RIM + count, wide), F32),
            vmem((RIM, wide), BF16),
            vmem((RIM, wide), BF16),
            vmem((count, width), F32),
            vmem((blocks * LANES, LANES), F32),
            vmem((blocks * LANES, LANES), F32),
            vmem(swap_shape, F32),
            vmem(swap_shape, BF16),
            vmem(swap_shape, BF16),
            vmem(swap_shape, BF16),
            vmem(swap_shape, BF16),
            vmem(back_shape, BF16),
            vmem(back_shape, BF16),
            vmem(flat_shape, F32),
            vmem(flat_shape, F32),
            vmem((groups, group * turn.shape[1], 2 * LANES), F32),
            vmem(back_shape[1:], F32),
            vmem((shards * group * blocks, LANES), F32),
            vmem((chans, groups, group * shards, count), BF16),
            vmem((chans, width, LANES), BF16),
            vmem((width, LANES), F32),
            vmem((groups, chans, group * shards, LANES), F32),
            vmem((groups, LANES, chans * group * shards), BF16),
            vmem((LANES, count), F32),
            vmem((LANES, LANES), F32),
            dma((14,)),
            dma((2, chunks + 1)), dma((chans, chunks + 1)), dma((chunks + 1,)),
            dma((3,)), dma((chans,)), dma, dma,
            dma((2,)), dma((2,)),
            dma((parts,)), dma((parts,)),
            dma((groups,)), dma((groups,)),
            dma((2, groups)), dma((chans, groups)), dma((groups,)),
        ],
        compiler_params=pltpu.CompilerParams(
            collective_id=0, has_side_effects=True, vmem_limit_bytes=56 * 1024 * 1024
        ),
        cost_estimate=pl.CostEstimate(flops=4 * 10**9, bytes_accessed=4 * 10**6, transcendentals=0),
    )(*operands)


def solution(mesh):
    shards, chans = mesh.shape["seq"], mesh.shape["chan"]
    return jax.shard_map(
        functools.partial(on_device, shards, chans),
        mesh=mesh,
        in_specs=(
            P("seq", "chan"),
            P(None, None, "chan"),
            P(None, None, "chan"),
            P("seq", "chan"),
            P("chan"),
            P("chan", None),
        ),
        out_specs=P("seq", "chan"),
        check_vma=False,
    )
```

```python
import functools
import math

import jax
import jax.numpy as jnp
import numpy as np
from jax import lax
from jax.experimental import pallas as pl
from jax.experimental.pallas import tpu as pltpu
from jax.sharding import PartitionSpec as P

MESH = pl.DeviceIdType.MESH
LANES = 128
RIM = 16
F32 = jnp.float32
BF16 = jnp.bfloat16


def split(values):
    high = values.astype(BF16)
    low = (values - high.astype(F32)).astype(BF16)
    return high, low


def split_table(table):
    table = np.asarray(table, np.float64)
    high = table.astype(np.float32).astype(BF16)
    low = (table - high.astype(np.float64)).astype(np.float32).astype(BF16)
    return high, low


def tables(total):
    first = total // LANES
    half = first // 2
    kept = half + 1
    padded = -(-kept // 16) * 16
    k1 = np.arange(padded)
    live = (k1 < kept).astype(np.float64)[:, None]
    n1 = np.arange(half)
    angle = 2.0 * math.pi / first * (k1[:, None] * n1[None, :] % first)
    outer = np.concatenate([np.cos(angle) * live, -np.sin(angle) * live], axis=0)
    outer_table = np.concatenate(split_table(outer), axis=1).astype(np.float32)
    n2 = np.arange(LANES)
    turn = 2.0 * math.pi / total * (k1[:, None] * n2[None, :] % total)
    turn_table = np.stack([np.cos(turn), -np.sin(turn)]).astype(np.float32)
    inner = 2.0 * math.pi / LANES * (n2[:, None] * n2[None, :] % LANES)
    cosine, sine = np.cos(inner), -np.sin(inner)
    ahead = np.block([[cosine, sine], [-sine, cosine]])
    ahead_table = ahead.astype(np.float32)
    back_table = ahead.T.astype(np.float32)
    weight = np.where((k1 == 0) | (k1 == half), 1.0, 2.0) * live[:, 0] / total
    close = np.concatenate([np.cos(angle).T * weight, -np.sin(angle).T * weight], axis=1)
    close_table = close.astype(np.float32)
    return outer_table, turn_table, ahead_table, back_table, close_table


def dot(left, right):
    return jnp.dot(left, right, preferred_element_type=F32)


def each(low, high, body):
    def one(i, carry):
        body(i)
        return carry

    lax.fori_loop(low, high, one, 0)


def piece(start, size):
    return pl.ds(pl.multiple_of(start, size), size)


def dot2(left, table_ref):
    rounded = left.astype(BF16)
    return dot(rounded, table_ref[0]) + dot(rounded, table_ref[1])


def kernel(
    shards, chans, chunks, parts, group,
    tok, w_in, sfilt_a, lfilt_a, gain_a, w_out, outer_a, turn_a, ahead_a, back_a, close_a,
    out,
    tbuf, tmini, w, sfilt, lfilt, gain, outer_f, turn_t, ahead_f, back_f, close_f,
    outer_t, ahead_t, back_t, close_t,
    proj, rim_out, rim_in, keep, keep_t, skip_t, stage, hs, hr, xs, xr, ys, yr,
    x32, h32, hspec, y32, c32, gbuf, wbuf, w32, w_rows, wt, acc, gain_rows,
    local, tok_send, tok_recv, fwd_send, wo_send, wo_recv, rim_send, rim_recv,
    h_send, h_recv, x_send, x_recv, y_send, y_recv, g_send, g_recv, gf_send,
):
    seq = lax.axis_index("seq")
    chan = lax.axis_index("chan")
    count = tok.shape[0]
    blocks = count // LANES
    cd = LANES // shards
    groups = cd // group
    rows = count // chunks
    core_peer = chan + 1 - 2 * (chan % 2)
    x_peer = (chan + 2) % chans
    diag = (core_peer + 2) % chans
    others = (core_peer, x_peer, diag)
    far_first = sorted(range(1, shards), key=lambda d: -min(d, shards - d))

    own_columns = pl.ds(pl.multiple_of(chan * LANES, LANES), LANES)
    loads = [(lfilt_a, lfilt), (tok, tbuf.at[chan]), (tok.at[pl.ds(count - RIM, RIM)], tmini.at[chan])]
    loads += [(w_in.at[g], w.at[:, pl.ds(g * LANES, LANES)]) for g in range(3)]
    loads += [(sfilt_a, sfilt), (gain_a, gain), (w_out.at[:, own_columns], wbuf.at[chan])]
    loads += [(outer_a, outer_f), (turn_a, turn_t), (ahead_a, ahead_f), (back_a, back_f), (close_a, close_f)]
    copies = [pltpu.make_async_copy(src, dst, local.at[i]) for i, (src, dst) in enumerate(loads)]
    for copy in copies:
        copy.start()

    barrier = pltpu.get_barrier_semaphore()
    for peer in others:
        pl.semaphore_signal(barrier, inc=1, device_id=(seq, peer), device_id_type=MESH)

    @functools.partial(each, 1, shards)
    def greet(d):
        peer = (seq + d) % shards
        pl.semaphore_signal(barrier, inc=1, device_id=(peer, chan), device_id_type=MESH)

    def spread(turned, block):
        for dest in range(shards):
            stage[dest, piece(block * cd, cd), :] = turned[dest * cd:(dest + 1) * cd, :]

    def pack(dst, part, pieces):
        size = blocks // pieces * cd
        span = piece(part * size, size)
        dst[:, span, :] = stage[:, span, :].astype(BF16)

    copies[0].wait()
    each(0, blocks, lambda block: spread(lfilt[piece(block * LANES, LANES), :].T, block))
    pack(hs, 0, 1)
    for copy in copies[1:]:
        copy.wait()
    gain_rows[...] = jnp.broadcast_to(gain[...], (LANES, LANES)).T
    outer_t[...] = outer_f[...].astype(BF16)
    for table, ref in ((ahead_f, ahead_t), (back_f, back_t), (close_f, close_t)):
        high, low = split(table[...])
        ref[0] = high
        ref[1] = low
    pl.semaphore_wait(barrier, len(others) + shards - 1)

    def remote(src, dst, send, recv, device):
        return pltpu.make_async_remote_copy(
            src_ref=src, dst_ref=dst, send_sem=send, recv_sem=recv,
            device_id=device, device_id_type=MESH,
        )

    def first(k):
        return isinstance(k, int) and k == 0

    def landing(k, owner):
        if first(k):
            return tmini.at[owner]
        return tbuf.at[owner, piece((k - 1) * rows, rows)]

    def tok_copy(k, slot, peer, owner):
        span = pl.ds(count - RIM, RIM) if first(k) else piece((k - 1) * rows, rows)
        return remote(tok.at[span], landing(k, owner), tok_send.at[slot, k], tok_recv.at[owner, k], (seq, peer))

    def fwd_copy(k, owner):
        return remote(landing(k, owner), landing(k, owner), fwd_send.at[k], tok_recv.at[owner, k], (seq, core_peer))

    def give(k):
        tok_copy(k, 1, x_peer, chan).start()
        tok_copy(k, 0, core_peer, chan).start()

    give(0)
    each(1, chunks + 1, give)

    def wo_copy(slot, peer, owner):
        columns = pl.ds(pl.multiple_of(peer * LANES, LANES), LANES)
        return remote(w_out.at[:, columns], wbuf.at[owner], wo_send.at[slot], wo_recv.at[owner], (seq, peer))

    def swap_all(action, src, dst, send, recv, part, span):
        if action == "start":
            for d in far_first:
                peer = (seq + d) % shards
                remote(src.at[peer, span], dst.at[seq, span], send.at[part], recv.at[part], (peer, chan)).start()
            return
        several = pl.ds(0, shards - 1)
        whole = remote(
            src.at[several, span], dst.at[several, span], send.at[part], recv.at[part], ((seq + 1) % shards, chan)
        )
        if action == "recv":
            whole.wait_recv()
        else:
            whole.wait_send()

    def h_swap(action):
        swap_all(action, hs, hr, h_send, h_recv, 0, pl.ds(0, blocks * cd))

    def x_swap(action, part):
        size = blocks // parts * cd
        swap_all(action, xs, xr, x_send, x_recv, part, piece(part * size, size))

    def y_swap(action, g):
        swap_all(action, ys.at[g], yr.at[g], y_send, y_recv, g, pl.ds(0, group * blocks))

    h_swap("start")
    hr[seq] = hs[seq]
    for slot, peer in enumerate(others):
        wo_copy(slot, peer, chan).start()

    def shorten(k):
        for g in range(3):
            lanes = slice(g * LANES, (g + 1) * LANES)
            base = pl.multiple_of(RIM // 2 + k * rows, 8)
            window = proj[pl.ds(base, rows + 8), lanes]
            value = (
                sfilt[0, g:g + 1, :] * window[8:, :]
                + sfilt[1, g:g + 1, :] * window[7:-1, :]
                + sfilt[2, g:g + 1, :] * window[6:-2, :]
            )
            if g == 0:
                held = value
            elif g == 1:
                held = held * value
            else:
                keep[piece(k * rows, rows), :] = value
        for j in range(rows // LANES):
            block = k * (rows // LANES) + j
            turned = held[j * LANES:(j + 1) * LANES, :].T
            spread(turned, block)
            skip_t[piece(block * LANES, LANES), :] = turned * gain_rows[...]

    def rim_copy():
        return remote(rim_out, rim_in, rim_send, rim_recv, ((seq + 1) % shards, chan))

    def take(k):
        tok_copy(k, 1, x_peer, x_peer).wait_recv()
        fwd_copy(k, x_peer).start()
        tok_copy(k, 0, core_peer, core_peer).wait_recv()
        tok_copy(k, 0, core_peer, diag).wait_recv()

    take(0)
    tail = jnp.concatenate([tmini[j] for j in range(chans)], axis=1)
    rim_out[...] = dot(tail, w[...]).astype(BF16)
    rim_copy().start()
    @functools.partial(each, 0, parts)
    def project(part):
        for i in range(chunks // parts):
            k = part * (chunks // parts) + i
            take(k + 1)
            span = piece(k * rows, rows)
            features = jnp.concatenate([tbuf[j, span, :] for j in range(chans)], axis=1)
            projected = dot(features, w[...]).astype(BF16)
            proj[pl.ds(pl.multiple_of(RIM + k * rows, RIM), rows), :] = projected.astype(F32)
            if i == 0:
                @pl.when(part == 0)
                def edge_rows():
                    rim_copy().wait_recv()
                    live = (seq > 0).astype(F32)
                    proj[0:RIM, :] = rim_in[...].astype(F32) * live
            shorten(k)
        pack(xs, part, parts)
        x_swap("start", part)

    xr[seq] = xs[seq]

    height = shards * blocks
    padded = turn_t.shape[1]
    edge = group * padded

    def spectrum(ref, g, product):
        columns = [ref[pl.ds(g * group + j, height, stride=cd), :].astype(BF16) for j in range(group)]
        signal = jnp.concatenate(columns, axis=1)
        signal = jnp.concatenate([signal, signal], axis=0)
        opened = dot(outer_t[...], signal)
        cosine, sine = turn_t[0], turn_t[1]
        turned = []
        for j in range(group):
            real = opened[:padded, j * LANES:(j + 1) * LANES]
            imag = opened[padded:, j * LANES:(j + 1) * LANES]
            turned.append(jnp.concatenate([real * cosine - imag * sine, real * sine + imag * cosine], axis=1))
        return product(jnp.concatenate(turned, axis=0), ahead_t)

    def dot1(left, table_ref):
        return dot(left.astype(BF16), table_ref[0])

    h_swap("recv")
    h32[...] = hr[...].reshape(h32.shape).astype(F32)

    @functools.partial(each, 0, groups)
    def filter_spectra(g):
        hspec[g] = spectrum(h32, g, dot2)

    @functools.partial(each, 0, blocks)
    def turn_gate(block):
        span = piece(block * LANES, LANES)
        keep_t[span, :] = keep[span, :].T

    for slot, peer in enumerate(others):
        wo_copy(slot, peer, peer).wait_recv()

    @functools.partial(each, 0, chans)
    def turn_weights(j):
        w32[...] = wbuf[j].astype(F32)
        for g in range(groups):
            picked = [w32[pl.ds(g * group + c, shards, stride=cd), :] for c in range(group)]
            w_rows[g, j] = jnp.concatenate(picked, axis=0)

    @functools.partial(each, 0, groups)
    def pack_weights(g):
        wt[g] = jnp.concatenate([w_rows[g, j] for j in range(chans)], axis=0).T.astype(BF16)

    def settle(k):
        tok_copy(k, 1, x_peer, chan).wait_send()
        tok_copy(k, 0, core_peer, chan).wait_send()
        fwd_copy(k, x_peer).wait_send()

    settle(0)
    each(1, chunks + 1, settle)
    acc[...] = jnp.zeros_like(acc)
    for slot, peer in enumerate(others):
        wo_copy(slot, peer, chan).wait_send()
    rim_copy().wait_send()
    h_swap("send")

    for part in range(parts):
        x_swap("recv", part)
    x32[...] = xr[...].reshape(x32.shape).astype(F32)

    def convolve(g):
        spectra = spectrum(x32, g, dot1)
        xr_, xi_ = spectra[:, :LANES], spectra[:, LANES:]
        hr_, hi_ = hspec[g, :, :LANES], hspec[g, :, LANES:]
        product = jnp.concatenate([xr_ * hr_ - xi_ * hi_, xr_ * hi_ + xi_ * hr_], axis=1)
        back = dot1(product, back_t)
        cosine, sine = turn_t[0], turn_t[1]
        sums = []
        for j in range(group):
            real = back[j * padded:(j + 1) * padded, :LANES]
            imag = back[j * padded:(j + 1) * padded, LANES:]
            sums.append(jnp.concatenate([real * cosine + imag * sine, imag * cosine - real * sine], axis=0))
        conv = dot(close_t[0], jnp.concatenate(sums, axis=1).astype(BF16))
        for j in range(group):
            y32[:, j * blocks:(j + 1) * blocks, :] = conv[:, j * LANES:(j + 1) * LANES].reshape(shards, blocks, LANES)
        ys[g] = y32[...].astype(BF16)
        y_swap("start", g)
        yr[g, seq] = ys[g, seq]

    def gated_copy(g, slot, peer, owner):
        return remote(gbuf.at[chan, g], gbuf.at[owner, g], g_send.at[slot, g], g_recv.at[owner, g], (seq, peer))

    def gated_fwd(g, owner):
        return remote(gbuf.at[owner, g], gbuf.at[owner, g], gf_send.at[g], g_recv.at[owner, g], (seq, core_peer))

    def gate(g):
        y_swap("recv", g)
        c32[...] = yr[g].reshape(c32.shape).astype(F32)
        for block in range(blocks):
            pieces = []
            for c in range(group):
                conv = c32[pl.ds(c * blocks + block, shards, stride=group * blocks), :]
                at = pl.ds(block * LANES + g * group + c, shards, stride=cd)
                pieces.append(keep_t[at, :] * (conv + skip_t[at, :]))
            gbuf[chan, g, :, block * LANES:(block + 1) * LANES] = jnp.concatenate(pieces, axis=0).astype(BF16)
        gated_copy(g, 1, x_peer, chan).start()
        gated_copy(g, 0, core_peer, chan).start()

    def forward(g):
        gated_copy(g, 1, x_peer, x_peer).wait_recv()
        gated_fwd(g, x_peer).start()

    def mix(g):
        gated_copy(g, 0, core_peer, core_peer).wait_recv()
        gated_copy(g, 0, core_peer, diag).wait_recv()
        whole = jnp.concatenate([gbuf[j, g] for j in range(chans)], axis=0)
        acc[...] += dot(wt[g], whole)

    @functools.partial(each, 0, groups + 1)
    def stream(g):
        pl.when(g < groups)(lambda: convolve(g))
        pl.when(g >= 1)(lambda: gate(g - 1))
        pl.when(g >= 2)(lambda: forward(g - 2))
        pl.when(g >= 3)(lambda: mix(g - 3))

    forward(groups - 1)
    each(0, parts, lambda part: x_swap("send", part))
    each(0, groups, lambda g: y_swap("send", g))
    each(max(groups - 2, 0), groups, mix)
    for block in range(blocks):
        span = slice(block * LANES, (block + 1) * LANES)
        out[span, :] = acc[:, span].T.astype(BF16)

    @functools.partial(each, 0, groups)
    def finish(g):
        gated_copy(g, 1, x_peer, chan).wait_send()
        gated_copy(g, 0, core_peer, chan).wait_send()
        gated_fwd(g, x_peer).wait_send()


def on_device(shards, chans, tokens, w_in, short_filter, long_filter, skip_gain, w_out):
    count, width = tokens.shape
    length = shards * count
    blocks = count // LANES
    cd = width // shards
    chunks = 4
    parts = 2
    group = min(cd, 8)
    groups = cd // group
    consts = tables(2 * length)
    outer, turn, ahead, back, close = consts
    wide = 3 * width
    inputs = w_in.shape[0]
    dma = pltpu.SemaphoreType.DMA
    vmem = pltpu.VMEM
    swap_shape = (shards, blocks * cd, LANES)
    flat_shape = (shards * blocks * cd, LANES)
    back_shape = (groups, shards, group * blocks, LANES)
    operands = (
        tokens, w_in.transpose(1, 0, 2), short_filter, long_filter,
        skip_gain.reshape(1, width), w_out,
    ) + tuple(jnp.asarray(c) for c in consts)
    return pl.pallas_call(
        functools.partial(kernel, shards, chans, chunks, parts, group),
        out_shape=jax.ShapeDtypeStruct((count, width), BF16),
        in_specs=[pl.BlockSpec(memory_space=pl.ANY)] * len(operands),
        out_specs=pl.BlockSpec(memory_space=vmem),
        scratch_shapes=[
            vmem((chans, count, width), BF16),
            vmem((chans, RIM, width), BF16),
            vmem((inputs, wide), BF16),
            vmem(short_filter.shape, F32),
            vmem((count, width), F32),
            vmem((1, width), F32),
        ] + [vmem(c.shape, F32) for c in consts] + [
            vmem(outer.shape, BF16),
            vmem((2,) + ahead.shape, BF16),
            vmem((2,) + back.shape, BF16),
            vmem((2,) + close.shape, BF16),
            vmem((RIM + count, wide), F32),
            vmem((RIM, wide), BF16),
            vmem((RIM, wide), BF16),
            vmem((count, width), F32),
            vmem((blocks * LANES, LANES), F32),
            vmem((blocks * LANES, LANES), F32),
            vmem(swap_shape, F32),
            vmem(swap_shape, BF16),
            vmem(swap_shape, BF16),
            vmem(swap_shape, BF16),
            vmem(swap_shape, BF16),
            vmem(back_shape, BF16),
            vmem(back_shape, BF16),
            vmem(flat_shape, F32),
            vmem(flat_shape, F32),
            vmem((groups, group * turn.shape[1], 2 * LANES), F32),
            vmem(back_shape[1:], F32),
            vmem((shards * group * blocks, LANES), F32),
            vmem((chans, groups, group * shards, count), BF16),
            vmem((chans, width, LANES), BF16),
            vmem((width, LANES), F32),
            vmem((groups, chans, group * shards, LANES), F32),
            vmem((groups, LANES, chans * group * shards), BF16),
            vmem((LANES, count), F32),
            vmem((LANES, LANES), F32),
            dma((14,)),
            dma((2, chunks + 1)), dma((chans, chunks + 1)), dma((chunks + 1,)),
            dma((3,)), dma((chans,)), dma, dma,
            dma((1,)), dma((1,)),
            dma((parts,)), dma((parts,)),
            dma((groups,)), dma((groups,)),
            dma((2, groups)), dma((chans, groups)), dma((groups,)),
        ],
        compiler_params=pltpu.CompilerParams(
            collective_id=0, has_side_effects=True, vmem_limit_bytes=56 * 1024 * 1024
        ),
        cost_estimate=pl.CostEstimate(flops=4 * 10**9, bytes_accessed=4 * 10**6, transcendentals=0),
    )(*operands)


def solution(mesh):
    shards, chans = mesh.shape["seq"], mesh.shape["chan"]
    return jax.shard_map(
        functools.partial(on_device, shards, chans),
        mesh=mesh,
        in_specs=(
            P("seq", "chan"),
            P(None, None, "chan"),
            P(None, None, "chan"),
            P("seq", "chan"),
            P("chan"),
            P("chan", None),
        ),
        out_specs=P("seq", "chan"),
        check_vma=False,
    )
```

```python
import functools
import math

import jax
import jax.numpy as jnp
import numpy as np
from jax import lax
from jax.experimental import pallas as pl
from jax.experimental.pallas import tpu as pltpu
from jax.sharding import PartitionSpec as P

MESH = pl.DeviceIdType.MESH
LANES = 128
RIM = 16
F32 = jnp.float32
BF16 = jnp.bfloat16


def split(values):
    high = values.astype(BF16)
    low = (values - high.astype(F32)).astype(BF16)
    return high, low


def split_table(table):
    table = np.asarray(table, np.float64)
    high = table.astype(np.float32).astype(BF16)
    low = (table - high.astype(np.float64)).astype(np.float32).astype(BF16)
    return high, low


def tables(total):
    first = total // LANES
    half = first // 2
    kept = half + 1
    padded = -(-kept // 16) * 16
    k1 = np.arange(padded)
    live = (k1 < kept).astype(np.float64)[:, None]
    n1 = np.arange(half)
    angle = 2.0 * math.pi / first * (k1[:, None] * n1[None, :] % first)
    outer = np.concatenate([np.cos(angle) * live, -np.sin(angle) * live], axis=0)
    outer_table = np.concatenate(split_table(outer), axis=1).astype(np.float32)
    n2 = np.arange(LANES)
    turn = 2.0 * math.pi / total * (k1[:, None] * n2[None, :] % total)
    turn_table = np.stack([np.cos(turn), -np.sin(turn)]).astype(np.float32)
    inner = 2.0 * math.pi / LANES * (n2[:, None] * n2[None, :] % LANES)
    cosine, sine = np.cos(inner), -np.sin(inner)
    ahead = np.block([[cosine, sine], [-sine, cosine]])
    ahead_table = ahead.astype(np.float32)
    back_table = ahead.T.astype(np.float32)
    weight = np.where((k1 == 0) | (k1 == half), 1.0, 2.0) * live[:, 0] / total
    close = np.concatenate([np.cos(angle).T * weight, -np.sin(angle).T * weight], axis=1)
    close_table = close.astype(np.float32)
    return outer_table, turn_table, ahead_table, back_table, close_table


def dot(left, right):
    return jnp.dot(left, right, preferred_element_type=F32)


def each(low, high, body):
    def one(i, carry):
        body(i)
        return carry

    lax.fori_loop(low, high, one, 0)


def piece(start, size):
    return pl.ds(pl.multiple_of(start, size), size)


def dot2(left, table_ref):
    rounded = left.astype(BF16)
    return dot(rounded, table_ref[0]) + dot(rounded, table_ref[1])


def kernel(
    shards, chans, chunks, parts, group,
    tok, w_in, sfilt_a, lfilt_a, gain_a, w_out, outer_a, turn_a, ahead_a, back_a, close_a,
    out,
    tbuf, tmini, w, sfilt, lfilt, gain, outer_f, turn_t, ahead_f, back_f, close_f,
    outer_t, ahead_t, back_t, close_t,
    proj, rim_out, rim_in, keep, keep_t, skip_t, stage, h_stage, hs, hr, xs, xr, ys, yr,
    x32, h32, hspec, y32, c32, gbuf, wbuf, w32, w_rows, wt, acc, gain_rows,
    local, tok_send, tok_recv, fwd_send, wo_send, wo_recv, rim_send, rim_recv,
    h_send, h_recv, x_send, x_recv, y_send, y_recv, g_send, g_recv, gf_send,
):
    seq = lax.axis_index("seq")
    chan = lax.axis_index("chan")
    count = tok.shape[0]
    blocks = count // LANES
    cd = LANES // shards
    groups = cd // group
    rows = count // chunks
    core_peer = chan + 1 - 2 * (chan % 2)
    x_peer = (chan + 2) % chans
    diag = (core_peer + 2) % chans
    others = (core_peer, x_peer, diag)
    far_first = sorted(range(1, shards), key=lambda d: -min(d, shards - d))

    own_columns = pl.ds(pl.multiple_of(chan * LANES, LANES), LANES)
    loads = [(lfilt_a, lfilt), (tok, tbuf.at[chan]), (tok.at[pl.ds(count - RIM, RIM)], tmini.at[chan])]
    loads += [(w_in.at[g], w.at[:, pl.ds(g * LANES, LANES)]) for g in range(3)]
    loads += [(sfilt_a, sfilt), (gain_a, gain), (w_out.at[:, own_columns], wbuf.at[chan])]
    loads += [(outer_a, outer_f), (turn_a, turn_t), (ahead_a, ahead_f), (back_a, back_f), (close_a, close_f)]
    copies = [pltpu.make_async_copy(src, dst, local.at[i]) for i, (src, dst) in enumerate(loads)]
    for copy in copies:
        copy.start()

    barrier = pltpu.get_barrier_semaphore()
    for peer in others:
        pl.semaphore_signal(barrier, inc=1, device_id=(seq, peer), device_id_type=MESH)

    @functools.partial(each, 1, shards)
    def greet(d):
        peer = (seq + d) % shards
        pl.semaphore_signal(barrier, inc=1, device_id=(peer, chan), device_id_type=MESH)

    def spread(turned, block):
        for dest in range(shards):
            stage[dest, piece(block * cd, cd), :] = turned[dest * cd:(dest + 1) * cd, :]

    def pack(dst, part, pieces):
        size = blocks // pieces * cd
        span = piece(part * size, size)
        dst[:, span, :] = stage[:, span, :].astype(BF16)

    copies[0].wait()
    @functools.partial(each, 0, blocks)
    def spread_filter(block):
        turned = lfilt[piece(block * LANES, LANES), :].T
        for dest in range(shards):
            for g in range(groups):
                start = dest * cd + g * group
                h_stage[g, dest, piece(block * group, group), :] = turned[start:start + group, :]

    hs[...] = h_stage[...].astype(BF16)
    for copy in copies[1:]:
        copy.wait()
    gain_rows[...] = jnp.broadcast_to(gain[...], (LANES, LANES)).T
    outer_t[...] = outer_f[...].astype(BF16)
    for table, ref in ((ahead_f, ahead_t), (back_f, back_t), (close_f, close_t)):
        high, low = split(table[...])
        ref[0] = high
        ref[1] = low
    pl.semaphore_wait(barrier, len(others) + shards - 1)

    def remote(src, dst, send, recv, device):
        return pltpu.make_async_remote_copy(
            src_ref=src, dst_ref=dst, send_sem=send, recv_sem=recv,
            device_id=device, device_id_type=MESH,
        )

    def first(k):
        return isinstance(k, int) and k == 0

    def landing(k, owner):
        if first(k):
            return tmini.at[owner]
        return tbuf.at[owner, piece((k - 1) * rows, rows)]

    def tok_copy(k, slot, peer, owner):
        span = pl.ds(count - RIM, RIM) if first(k) else piece((k - 1) * rows, rows)
        return remote(tok.at[span], landing(k, owner), tok_send.at[slot, k], tok_recv.at[owner, k], (seq, peer))

    def fwd_copy(k, owner):
        return remote(landing(k, owner), landing(k, owner), fwd_send.at[k], tok_recv.at[owner, k], (seq, core_peer))

    def give(k):
        tok_copy(k, 1, x_peer, chan).start()
        tok_copy(k, 0, core_peer, chan).start()

    give(0)
    each(1, chunks + 1, give)

    def wo_copy(slot, peer, owner):
        columns = pl.ds(pl.multiple_of(peer * LANES, LANES), LANES)
        return remote(w_out.at[:, columns], wbuf.at[owner], wo_send.at[slot], wo_recv.at[owner], (seq, peer))

    def swap_all(action, src, dst, send, recv, part, span):
        if action == "start":
            for d in far_first:
                peer = (seq + d) % shards
                remote(src.at[peer, span], dst.at[seq, span], send.at[part], recv.at[part], (peer, chan)).start()
            return
        several = pl.ds(0, shards - 1)
        whole = remote(
            src.at[several, span], dst.at[several, span], send.at[part], recv.at[part], ((seq + 1) % shards, chan)
        )
        if action == "recv":
            whole.wait_recv()
        else:
            whole.wait_send()

    def h_swap(action, g):
        swap_all(action, hs.at[g], hr.at[g], h_send, h_recv, g, pl.ds(0, blocks * group))

    def x_swap(action, part):
        size = blocks // parts * cd
        swap_all(action, xs, xr, x_send, x_recv, part, piece(part * size, size))

    def y_swap(action, g):
        swap_all(action, ys.at[g], yr.at[g], y_send, y_recv, g, pl.ds(0, group * blocks))

    h_swap("start", 0)
    for g in range(groups):
        hr[g, seq] = hs[g, seq]
    for slot, peer in enumerate(others):
        wo_copy(slot, peer, chan).start()

    def shorten(k):
        for g in range(3):
            lanes = slice(g * LANES, (g + 1) * LANES)
            base = pl.multiple_of(RIM // 2 + k * rows, 8)
            window = proj[pl.ds(base, rows + 8), lanes]
            value = (
                sfilt[0, g:g + 1, :] * window[8:, :]
                + sfilt[1, g:g + 1, :] * window[7:-1, :]
                + sfilt[2, g:g + 1, :] * window[6:-2, :]
            )
            if g == 0:
                held = value
            elif g == 1:
                held = held * value
            else:
                keep[piece(k * rows, rows), :] = value
        for j in range(rows // LANES):
            block = k * (rows // LANES) + j
            turned = held[j * LANES:(j + 1) * LANES, :].T
            spread(turned, block)
            skip_t[piece(block * LANES, LANES), :] = turned * gain_rows[...]

    def rim_copy():
        return remote(rim_out, rim_in, rim_send, rim_recv, ((seq + 1) % shards, chan))

    def take(k):
        tok_copy(k, 1, x_peer, x_peer).wait_recv()
        fwd_copy(k, x_peer).start()
        tok_copy(k, 0, core_peer, core_peer).wait_recv()
        tok_copy(k, 0, core_peer, diag).wait_recv()

    take(0)
    tail = jnp.concatenate([tmini[j] for j in range(chans)], axis=1)
    rim_out[...] = dot(tail, w[...]).astype(BF16)
    rim_copy().start()
    @functools.partial(each, 0, parts)
    def project(part):
        for i in range(chunks // parts):
            k = part * (chunks // parts) + i
            take(k + 1)
            span = piece(k * rows, rows)
            features = jnp.concatenate([tbuf[j, span, :] for j in range(chans)], axis=1)
            projected = dot(features, w[...]).astype(BF16)
            proj[pl.ds(pl.multiple_of(RIM + k * rows, RIM), rows), :] = projected.astype(F32)
            if i == 0:
                @pl.when(part == 0)
                def edge_rows():
                    rim_copy().wait_recv()
                    live = (seq > 0).astype(F32)
                    proj[0:RIM, :] = rim_in[...].astype(F32) * live
            shorten(k)
        pack(xs, part, parts)
        x_swap("start", part)
        for j in range(blocks // parts):
            span = piece((part * (blocks // parts) + j) * LANES, LANES)
            keep_t[span, :] = keep[span, :].T

    for g in range(1, groups):
        h_swap("start", g)
    xr[seq] = xs[seq]

    height = shards * blocks
    padded = turn_t.shape[1]
    edge = group * padded

    def spectrum(ref, start, stride, product):
        columns = [ref[pl.ds(start + j, height, stride=stride), :].astype(BF16) for j in range(group)]
        signal = jnp.concatenate(columns, axis=1)
        signal = jnp.concatenate([signal, signal], axis=0)
        opened = dot(outer_t[...], signal)
        cosine, sine = turn_t[0], turn_t[1]
        turned = []
        for j in range(group):
            real = opened[:padded, j * LANES:(j + 1) * LANES]
            imag = opened[padded:, j * LANES:(j + 1) * LANES]
            turned.append(jnp.concatenate([real * cosine - imag * sine, real * sine + imag * cosine], axis=1))
        return product(jnp.concatenate(turned, axis=0), ahead_t)

    def dot1(left, table_ref):
        return dot(left.astype(BF16), table_ref[0])

    def filter_spectra(g):
        h_swap("recv", g)
        h32[...] = hr[g].reshape(h32.shape).astype(F32)
        hspec[g] = spectrum(h32, 0, group, dot2)

    filter_spectra(0)
    acc[...] = jnp.zeros_like(acc)

    for part in range(parts):
        x_swap("recv", part)
    x32[...] = xr[...].reshape(x32.shape).astype(F32)

    def convolve(g):
        spectra = spectrum(x32, g * group, cd, dot1)
        xr_, xi_ = spectra[:, :LANES], spectra[:, LANES:]
        hr_, hi_ = hspec[g, :, :LANES], hspec[g, :, LANES:]
        product = jnp.concatenate([xr_ * hr_ - xi_ * hi_, xr_ * hi_ + xi_ * hr_], axis=1)
        back = dot1(product, back_t)
        cosine, sine = turn_t[0], turn_t[1]
        sums = []
        for j in range(group):
            real = back[j * padded:(j + 1) * padded, :LANES]
            imag = back[j * padded:(j + 1) * padded, LANES:]
            sums.append(jnp.concatenate([real * cosine + imag * sine, imag * cosine - real * sine], axis=0))
        conv = dot(close_t[0], jnp.concatenate(sums, axis=1).astype(BF16))
        for j in range(group):
            y32[:, j * blocks:(j + 1) * blocks, :] = conv[:, j * LANES:(j + 1) * LANES].reshape(shards, blocks, LANES)
        ys[g] = y32[...].astype(BF16)
        y_swap("start", g)
        yr[g, seq] = ys[g, seq]

    def gated_copy(g, slot, peer, owner):
        return remote(gbuf.at[chan, g], gbuf.at[owner, g], g_send.at[slot, g], g_recv.at[owner, g], (seq, peer))

    def gated_fwd(g, owner):
        return remote(gbuf.at[owner, g], gbuf.at[owner, g], gf_send.at[g], g_recv.at[owner, g], (seq, core_peer))

    def gate(g):
        y_swap("recv", g)
        c32[...] = yr[g].reshape(c32.shape).astype(F32)
        for block in range(blocks):
            pieces = []
            for c in range(group):
                conv = c32[pl.ds(c * blocks + block, shards, stride=group * blocks), :]
                at = pl.ds(block * LANES + g * group + c, shards, stride=cd)
                pieces.append(keep_t[at, :] * (conv + skip_t[at, :]))
            gbuf[chan, g, :, block * LANES:(block + 1) * LANES] = jnp.concatenate(pieces, axis=0).astype(BF16)
        gated_copy(g, 1, x_peer, chan).start()
        gated_copy(g, 0, core_peer, chan).start()

    def forward(g):
        gated_copy(g, 1, x_peer, x_peer).wait_recv()
        gated_fwd(g, x_peer).start()

    def mix(g):
        gated_copy(g, 0, core_peer, core_peer).wait_recv()
        gated_copy(g, 0, core_peer, diag).wait_recv()
        whole = jnp.concatenate([gbuf[j, g] for j in range(chans)], axis=0)
        acc[...] += dot(wt[g], whole)

    def meanwhile():
        for slot, peer in enumerate(others):
            wo_copy(slot, peer, peer).wait_recv()

        @functools.partial(each, 0, chans)
        def turn_weights(j):
            w32[...] = wbuf[j].astype(F32)
            for g in range(groups):
                picked = [w32[pl.ds(g * group + c, shards, stride=cd), :] for c in range(group)]
                w_rows[g, j] = jnp.concatenate(picked, axis=0)

        @functools.partial(each, 0, groups)
        def pack_weights(g):
            wt[g] = jnp.concatenate([w_rows[g, j] for j in range(chans)], axis=0).T.astype(BF16)

        def settle(k):
            tok_copy(k, 1, x_peer, chan).wait_send()
            tok_copy(k, 0, core_peer, chan).wait_send()
            fwd_copy(k, x_peer).wait_send()

        settle(0)
        each(1, chunks + 1, settle)
        for slot, peer in enumerate(others):
            wo_copy(slot, peer, chan).wait_send()
        rim_copy().wait_send()
        each(0, groups, lambda g: h_swap("send", g))

    @functools.partial(each, 0, groups + 1)
    def stream(g):
        pl.when((g >= 1) & (g < groups))(lambda: filter_spectra(g))
        pl.when(g < groups)(lambda: convolve(g))
        pl.when(g >= 1)(lambda: gate(g - 1))
        pl.when(g >= 2)(lambda: forward(g - 2))
        pl.when(g == groups - 1)(meanwhile)
        pl.when(g >= 3)(lambda: mix(g - 3))

    forward(groups - 1)
    each(0, parts, lambda part: x_swap("send", part))
    each(0, groups, lambda g: y_swap("send", g))
    each(max(groups - 2, 0), groups, mix)
    for block in range(blocks):
        span = slice(block * LANES, (block + 1) * LANES)
        out[span, :] = acc[:, span].T

    @functools.partial(each, 0, groups)
    def finish(g):
        gated_copy(g, 1, x_peer, chan).wait_send()
        gated_copy(g, 0, core_peer, chan).wait_send()
        gated_fwd(g, x_peer).wait_send()


def on_device(shards, chans, tokens, w_in, short_filter, long_filter, skip_gain, w_out):
    count, width = tokens.shape
    length = shards * count
    blocks = count // LANES
    cd = width // shards
    chunks = 4
    parts = 2
    group = min(cd, 8)
    groups = cd // group
    consts = tables(2 * length)
    outer, turn, ahead, back, close = consts
    wide = 3 * width
    inputs = w_in.shape[0]
    dma = pltpu.SemaphoreType.DMA
    vmem = pltpu.VMEM
    swap_shape = (shards, blocks * cd, LANES)
    flat_shape = (shards * blocks * cd, LANES)
    back_shape = (groups, shards, group * blocks, LANES)
    operands = (
        tokens, w_in.transpose(1, 0, 2), short_filter, long_filter,
        skip_gain.reshape(1, width), w_out,
    ) + tuple(jnp.asarray(c) for c in consts)
    return pl.pallas_call(
        functools.partial(kernel, shards, chans, chunks, parts, group),
        out_shape=jax.ShapeDtypeStruct((count, width), F32),
        in_specs=[pl.BlockSpec(memory_space=pl.ANY)] * len(operands),
        out_specs=pl.BlockSpec(memory_space=vmem),
        scratch_shapes=[
            vmem((chans, count, width), BF16),
            vmem((chans, RIM, width), BF16),
            vmem((inputs, wide), BF16),
            vmem(short_filter.shape, F32),
            vmem((count, width), F32),
            vmem((1, width), F32),
        ] + [vmem(c.shape, F32) for c in consts] + [
            vmem(outer.shape, BF16),
            vmem((2,) + ahead.shape, BF16),
            vmem((2,) + back.shape, BF16),
            vmem((2,) + close.shape, BF16),
            vmem((RIM + count, wide), F32),
            vmem((RIM, wide), BF16),
            vmem((RIM, wide), BF16),
            vmem((count, width), F32),
            vmem((blocks * LANES, LANES), F32),
            vmem((blocks * LANES, LANES), F32),
            vmem(swap_shape, F32),
            vmem(back_shape, F32),
            vmem(back_shape, BF16),
            vmem(back_shape, BF16),
            vmem(swap_shape, BF16),
            vmem(swap_shape, BF16),
            vmem(back_shape, BF16),
            vmem(back_shape, BF16),
            vmem(flat_shape, F32),
            vmem((shards * group * blocks, LANES), F32),
            vmem((groups, group * turn.shape[1], 2 * LANES), F32),
            vmem(back_shape[1:], F32),
            vmem((shards * group * blocks, LANES), F32),
            vmem((chans, groups, group * shards, count), BF16),
            vmem((chans, width, LANES), BF16),
            vmem((width, LANES), F32),
            vmem((groups, chans, group * shards, LANES), F32),
            vmem((groups, LANES, chans * group * shards), BF16),
            vmem((LANES, count), F32),
            vmem((LANES, LANES), F32),
            dma((14,)),
            dma((2, chunks + 1)), dma((chans, chunks + 1)), dma((chunks + 1,)),
            dma((3,)), dma((chans,)), dma, dma,
            dma((groups,)), dma((groups,)),
            dma((parts,)), dma((parts,)),
            dma((groups,)), dma((groups,)),
            dma((2, groups)), dma((chans, groups)), dma((groups,)),
        ],
        compiler_params=pltpu.CompilerParams(
            collective_id=0, has_side_effects=True, vmem_limit_bytes=56 * 1024 * 1024
        ),
        cost_estimate=pl.CostEstimate(flops=4 * 10**9, bytes_accessed=4 * 10**6, transcendentals=0),
    )(*operands).astype(BF16)


def solution(mesh):
    shards, chans = mesh.shape["seq"], mesh.shape["chan"]
    return jax.shard_map(
        functools.partial(on_device, shards, chans),
        mesh=mesh,
        in_specs=(
            P("seq", "chan"),
            P(None, None, "chan"),
            P(None, None, "chan"),
            P("seq", "chan"),
            P("chan"),
            P("chan", None),
        ),
        out_specs=P("seq", "chan"),
        check_vma=False,
    )
```

```python
import functools
import math

import jax
import jax.numpy as jnp
import numpy as np
from jax import lax
from jax.experimental import pallas as pl
from jax.experimental.pallas import tpu as pltpu
from jax.sharding import PartitionSpec as P

MESH = pl.DeviceIdType.MESH
LANES = 128
RIM = 16
F32 = jnp.float32
BF16 = jnp.bfloat16


def split(values):
    high = values.astype(BF16)
    low = (values - high.astype(F32)).astype(BF16)
    return high, low


def split_table(table):
    table = np.asarray(table, np.float64)
    high = table.astype(np.float32).astype(BF16)
    low = (table - high.astype(np.float64)).astype(np.float32).astype(BF16)
    return high, low


def tables(total):
    first = total // LANES
    half = first // 2
    kept = half + 1
    padded = -(-kept // 16) * 16
    k1 = np.arange(padded)
    live = (k1 < kept).astype(np.float64)[:, None]
    n1 = np.arange(half)
    angle = 2.0 * math.pi / first * (k1[:, None] * n1[None, :] % first)
    outer = np.concatenate([np.cos(angle) * live, -np.sin(angle) * live], axis=0)
    outer_table = np.concatenate(split_table(outer), axis=1).astype(np.float32)
    n2 = np.arange(LANES)
    turn = 2.0 * math.pi / total * (k1[:, None] * n2[None, :] % total)
    turn_table = np.stack([np.cos(turn), -np.sin(turn)]).astype(np.float32)
    inner = 2.0 * math.pi / LANES * (n2[:, None] * n2[None, :] % LANES)
    cosine, sine = np.cos(inner), -np.sin(inner)
    ahead = np.block([[cosine, sine], [-sine, cosine]])
    ahead_table = ahead.astype(np.float32)
    back_table = ahead.T.astype(np.float32)
    weight = np.where((k1 == 0) | (k1 == half), 1.0, 2.0) * live[:, 0] / total
    close = np.concatenate([np.cos(angle).T * weight, -np.sin(angle).T * weight], axis=1)
    close_table = close.astype(np.float32)
    return outer_table, turn_table, ahead_table, back_table, close_table


def dot(left, right):
    return jnp.dot(left, right, preferred_element_type=F32)


def each(low, high, body):
    def one(i, carry):
        body(i)
        return carry

    lax.fori_loop(low, high, one, 0)


def piece(start, size):
    return pl.ds(pl.multiple_of(start, size), size)


def dot2(left, table_ref):
    rounded = left.astype(BF16)
    return dot(rounded, table_ref[0]) + dot(rounded, table_ref[1])


def kernel(
    shards, chans, chunks, parts, group, many,
    tok, w_in, sfilt_a, lfilt_a, gain_a, w_out, outer_a, turn_a, ahead_a, back_a, close_a,
    out,
    tbuf, tmini, w, sfilt, lfilt, gain, outer_f, turn_t, ahead_f, back_f, close_f,
    outer_t, ahead_t, back_t, close_t,
    proj, rim_out, rim_in, keep, keep_t, skip_t, stage, h_stage, hs, hr, xs, xr, ys, yr,
    x32, h32, hspec, y32, c32, gbuf, wbuf, w32, w_rows, wt, acc, gain_rows,
    local, tok_send, tok_recv, fwd_send, wo_send, wo_recv, rim_send, rim_recv,
    h_send, h_recv, x_send, x_recv, y_send, y_recv, g_send, g_recv, gf_send,
):
    seq = lax.axis_index("seq")
    chan = lax.axis_index("chan")
    count = tok.shape[0]
    blocks = count // LANES
    cd = LANES // shards
    groups = cd // group
    lots = cd // many
    per = many // group
    rows = count // chunks
    core_peer = chan + 1 - 2 * (chan % 2)
    x_peer = (chan + 2) % chans
    diag = (core_peer + 2) % chans
    others = (core_peer, x_peer, diag)
    far_first = sorted(range(1, shards), key=lambda d: -min(d, shards - d))

    own_columns = pl.ds(pl.multiple_of(chan * LANES, LANES), LANES)
    loads = [(lfilt_a, lfilt), (tok, tbuf.at[chan]), (tok.at[pl.ds(count - RIM, RIM)], tmini.at[chan])]
    loads += [(w_in.at[g], w.at[:, pl.ds(g * LANES, LANES)]) for g in range(3)]
    loads += [(sfilt_a, sfilt), (gain_a, gain), (w_out.at[:, own_columns], wbuf.at[chan])]
    loads += [(outer_a, outer_f), (turn_a, turn_t), (ahead_a, ahead_f), (back_a, back_f), (close_a, close_f)]
    copies = [pltpu.make_async_copy(src, dst, local.at[i]) for i, (src, dst) in enumerate(loads)]
    for copy in copies:
        copy.start()

    barrier = pltpu.get_barrier_semaphore()
    for peer in others:
        pl.semaphore_signal(barrier, inc=1, device_id=(seq, peer), device_id_type=MESH)

    @functools.partial(each, 1, shards)
    def greet(d):
        peer = (seq + d) % shards
        pl.semaphore_signal(barrier, inc=1, device_id=(peer, chan), device_id_type=MESH)

    def spread(turned, block):
        for dest in range(shards):
            stage[dest, piece(block * cd, cd), :] = turned[dest * cd:(dest + 1) * cd, :]

    def pack(dst, part, pieces):
        size = blocks // pieces * cd
        span = piece(part * size, size)
        dst[:, span, :] = stage[:, span, :].astype(BF16)

    copies[0].wait()
    @functools.partial(each, 0, blocks)
    def spread_filter(block):
        turned = lfilt[piece(block * LANES, LANES), :].T
        for dest in range(shards):
            for g in range(lots):
                start = dest * cd + g * many
                h_stage[g, dest, piece(block * many, many), :] = turned[start:start + many, :]

    hs[...] = h_stage[...].astype(BF16)
    for copy in copies[1:]:
        copy.wait()
    gain_rows[...] = jnp.broadcast_to(gain[...], (LANES, LANES)).T
    outer_t[...] = outer_f[...].astype(BF16)
    for table, ref in ((ahead_f, ahead_t), (back_f, back_t), (close_f, close_t)):
        high, low = split(table[...])
        ref[0] = high
        ref[1] = low
    pl.semaphore_wait(barrier, len(others) + shards - 1)

    def remote(src, dst, send, recv, device):
        return pltpu.make_async_remote_copy(
            src_ref=src, dst_ref=dst, send_sem=send, recv_sem=recv,
            device_id=device, device_id_type=MESH,
        )

    def first(k):
        return isinstance(k, int) and k == 0

    def landing(k, owner):
        if first(k):
            return tmini.at[owner]
        return tbuf.at[owner, piece((k - 1) * rows, rows)]

    def tok_copy(k, slot, peer, owner):
        span = pl.ds(count - RIM, RIM) if first(k) else piece((k - 1) * rows, rows)
        return remote(tok.at[span], landing(k, owner), tok_send.at[slot, k], tok_recv.at[owner, k], (seq, peer))

    def fwd_copy(k, owner):
        return remote(landing(k, owner), landing(k, owner), fwd_send.at[k], tok_recv.at[owner, k], (seq, core_peer))

    def give(k):
        tok_copy(k, 1, x_peer, chan).start()
        tok_copy(k, 0, core_peer, chan).start()

    give(0)
    each(1, chunks + 1, give)

    def wo_copy(slot, peer, owner):
        columns = pl.ds(pl.multiple_of(peer * LANES, LANES), LANES)
        return remote(w_out.at[:, columns], wbuf.at[owner], wo_send.at[slot], wo_recv.at[owner], (seq, peer))

    def swap_all(action, src, dst, send, recv, part, span):
        if action == "start":
            for d in far_first:
                peer = (seq + d) % shards
                remote(src.at[peer, span], dst.at[seq, span], send.at[part], recv.at[part], (peer, chan)).start()
            return
        several = pl.ds(0, shards - 1)
        whole = remote(
            src.at[several, span], dst.at[several, span], send.at[part], recv.at[part], ((seq + 1) % shards, chan)
        )
        if action == "recv":
            whole.wait_recv()
        else:
            whole.wait_send()

    def h_swap(action, g):
        swap_all(action, hs.at[g], hr.at[g], h_send, h_recv, g, pl.ds(0, blocks * many))

    def x_swap(action, part):
        size = blocks // parts * cd
        swap_all(action, xs, xr, x_send, x_recv, part, piece(part * size, size))

    def y_swap(action, g):
        swap_all(action, ys.at[g], yr.at[g], y_send, y_recv, g, pl.ds(0, group * blocks))

    h_swap("start", 0)
    for g in range(lots):
        hr[g, seq] = hs[g, seq]
    for slot, peer in enumerate(others):
        wo_copy(slot, peer, chan).start()

    def shorten(k):
        for g in range(3):
            lanes = slice(g * LANES, (g + 1) * LANES)
            base = pl.multiple_of(RIM // 2 + k * rows, 8)
            window = proj[pl.ds(base, rows + 8), lanes]
            value = (
                sfilt[0, g:g + 1, :] * window[8:, :]
                + sfilt[1, g:g + 1, :] * window[7:-1, :]
                + sfilt[2, g:g + 1, :] * window[6:-2, :]
            )
            if g == 0:
                held = value
            elif g == 1:
                held = held * value
            else:
                keep[piece(k * rows, rows), :] = value
        for j in range(rows // LANES):
            block = k * (rows // LANES) + j
            turned = held[j * LANES:(j + 1) * LANES, :].T
            spread(turned, block)
            skip_t[piece(block * LANES, LANES), :] = turned * gain_rows[...]

    def rim_copy():
        return remote(rim_out, rim_in, rim_send, rim_recv, ((seq + 1) % shards, chan))

    def take(k):
        tok_copy(k, 1, x_peer, x_peer).wait_recv()
        fwd_copy(k, x_peer).start()
        tok_copy(k, 0, core_peer, core_peer).wait_recv()
        tok_copy(k, 0, core_peer, diag).wait_recv()

    take(0)
    tail = jnp.concatenate([tmini[j] for j in range(chans)], axis=1)
    rim_out[...] = dot(tail, w[...]).astype(BF16)
    rim_copy().start()
    @functools.partial(each, 0, parts)
    def project(part):
        for i in range(chunks // parts):
            k = part * (chunks // parts) + i
            take(k + 1)
            span = piece(k * rows, rows)
            features = jnp.concatenate([tbuf[j, span, :] for j in range(chans)], axis=1)
            projected = dot(features, w[...]).astype(BF16)
            proj[pl.ds(pl.multiple_of(RIM + k * rows, RIM), rows), :] = projected.astype(F32)
            if i == 0:
                @pl.when(part == 0)
                def edge_rows():
                    rim_copy().wait_recv()
                    live = (seq > 0).astype(F32)
                    proj[0:RIM, :] = rim_in[...].astype(F32) * live
            shorten(k)
        pack(xs, part, parts)
        x_swap("start", part)
        for j in range(blocks // parts):
            span = piece((part * (blocks // parts) + j) * LANES, LANES)
            keep_t[span, :] = keep[span, :].T

    for g in range(1, lots):
        h_swap("start", g)
    xr[seq] = xs[seq]

    height = shards * blocks
    padded = turn_t.shape[1]
    edge = group * padded

    def spectrum(ref, start, size, stride, product):
        columns = [ref[pl.ds(start + j, height, stride=stride), :].astype(BF16) for j in range(size)]
        signal = jnp.concatenate(columns, axis=1)
        signal = jnp.concatenate([signal, signal], axis=0)
        opened = dot(outer_t[...], signal)
        cosine, sine = turn_t[0], turn_t[1]
        turned = []
        for j in range(size):
            real = opened[:padded, j * LANES:(j + 1) * LANES]
            imag = opened[padded:, j * LANES:(j + 1) * LANES]
            turned.append(jnp.concatenate([real * cosine - imag * sine, real * sine + imag * cosine], axis=1))
        return product(jnp.concatenate(turned, axis=0), ahead_t)

    def dot1(left, table_ref):
        return dot(left.astype(BF16), table_ref[0])

    def filter_spectra(g):
        h_swap("recv", g)
        h32[...] = hr[g].reshape(h32.shape).astype(F32)
        hspec[g] = spectrum(h32, 0, many, many, dot2)

    filter_spectra(0)
    acc[...] = jnp.zeros_like(acc)

    for part in range(parts):
        x_swap("recv", part)
    x32[...] = xr[...].reshape(x32.shape).astype(F32)

    def convolve(g):
        spectra = spectrum(x32, g * group, group, cd, dot1)
        xr_, xi_ = spectra[:, :LANES], spectra[:, LANES:]
        at = piece(g % per * edge, edge)
        hr_, hi_ = hspec[g // per, at, :LANES], hspec[g // per, at, LANES:]
        product = jnp.concatenate([xr_ * hr_ - xi_ * hi_, xr_ * hi_ + xi_ * hr_], axis=1)
        back = dot1(product, back_t)
        cosine, sine = turn_t[0], turn_t[1]
        sums = []
        for j in range(group):
            real = back[j * padded:(j + 1) * padded, :LANES]
            imag = back[j * padded:(j + 1) * padded, LANES:]
            sums.append(jnp.concatenate([real * cosine + imag * sine, imag * cosine - real * sine], axis=0))
        conv = dot(close_t[0], jnp.concatenate(sums, axis=1).astype(BF16))
        for j in range(group):
            y32[:, j * blocks:(j + 1) * blocks, :] = conv[:, j * LANES:(j + 1) * LANES].reshape(shards, blocks, LANES)
        ys[g] = y32[...].astype(BF16)
        y_swap("start", g)
        yr[g, seq] = ys[g, seq]

    def gated_copy(g, slot, peer, owner):
        return remote(gbuf.at[chan, g], gbuf.at[owner, g], g_send.at[slot, g], g_recv.at[owner, g], (seq, peer))

    def gated_fwd(g, owner):
        return remote(gbuf.at[owner, g], gbuf.at[owner, g], gf_send.at[g], g_recv.at[owner, g], (seq, core_peer))

    def gate(g):
        y_swap("recv", g)
        c32[...] = yr[g].reshape(c32.shape).astype(F32)
        for block in range(blocks):
            pieces = []
            for c in range(group):
                conv = c32[pl.ds(c * blocks + block, shards, stride=group * blocks), :]
                at = pl.ds(block * LANES + g * group + c, shards, stride=cd)
                pieces.append(keep_t[at, :] * (conv + skip_t[at, :]))
            gbuf[chan, g, :, block * LANES:(block + 1) * LANES] = jnp.concatenate(pieces, axis=0).astype(BF16)
        gated_copy(g, 1, x_peer, chan).start()
        gated_copy(g, 0, core_peer, chan).start()

    def forward(g):
        gated_copy(g, 1, x_peer, x_peer).wait_recv()
        gated_fwd(g, x_peer).start()

    def mix(g):
        gated_copy(g, 0, core_peer, core_peer).wait_recv()
        gated_copy(g, 0, core_peer, diag).wait_recv()
        whole = jnp.concatenate([gbuf[j, g] for j in range(chans)], axis=0)
        acc[...] += dot(wt[g], whole)

    def meanwhile():
        for slot, peer in enumerate(others):
            wo_copy(slot, peer, peer).wait_recv()

        @functools.partial(each, 0, chans)
        def turn_weights(j):
            w32[...] = wbuf[j].astype(F32)
            for g in range(groups):
                picked = [w32[pl.ds(g * group + c, shards, stride=cd), :] for c in range(group)]
                w_rows[g, j] = jnp.concatenate(picked, axis=0)

        @functools.partial(each, 0, groups)
        def pack_weights(g):
            wt[g] = jnp.concatenate([w_rows[g, j] for j in range(chans)], axis=0).T.astype(BF16)

        def settle(k):
            tok_copy(k, 1, x_peer, chan).wait_send()
            tok_copy(k, 0, core_peer, chan).wait_send()
            fwd_copy(k, x_peer).wait_send()

        settle(0)
        each(1, chunks + 1, settle)
        for slot, peer in enumerate(others):
            wo_copy(slot, peer, chan).wait_send()
        rim_copy().wait_send()
        each(0, lots, lambda g: h_swap("send", g))

    @functools.partial(each, 0, groups + 1)
    def stream(g):
        pl.when((g >= 1) & (g < groups) & (g % per == 0))(lambda: filter_spectra(g // per))
        pl.when(g < groups)(lambda: convolve(g))
        pl.when(g >= 1)(lambda: gate(g - 1))
        pl.when(g >= 2)(lambda: forward(g - 2))
        pl.when(g == groups - 1)(meanwhile)
        pl.when(g >= 3)(lambda: mix(g - 3))

    forward(groups - 1)
    each(0, parts, lambda part: x_swap("send", part))
    each(0, groups, lambda g: y_swap("send", g))
    each(max(groups - 2, 0), groups, mix)
    for block in range(blocks):
        span = slice(block * LANES, (block + 1) * LANES)
        out[span, :] = acc[:, span].T.astype(BF16)

    @functools.partial(each, 0, groups)
    def finish(g):
        gated_copy(g, 1, x_peer, chan).wait_send()
        gated_copy(g, 0, core_peer, chan).wait_send()
        gated_fwd(g, x_peer).wait_send()


def on_device(shards, chans, tokens, w_in, short_filter, long_filter, skip_gain, w_out):
    count, width = tokens.shape
    length = shards * count
    blocks = count // LANES
    cd = width // shards
    chunks = 8
    parts = 4 if blocks // 4 * cd % 16 == 0 else 2
    group = min(cd, 4)
    many = min(cd, 8)
    groups = cd // group
    consts = tables(2 * length)
    outer, turn, ahead, back, close = consts
    wide = 3 * width
    inputs = w_in.shape[0]
    dma = pltpu.SemaphoreType.DMA
    vmem = pltpu.VMEM
    swap_shape = (shards, blocks * cd, LANES)
    flat_shape = (shards * blocks * cd, LANES)
    back_shape = (groups, shards, group * blocks, LANES)
    filter_shape = (cd // many, shards, many * blocks, LANES)
    operands = (
        tokens, w_in.transpose(1, 0, 2), short_filter, long_filter,
        skip_gain.reshape(1, width), w_out,
    ) + tuple(jnp.asarray(c) for c in consts)
    return pl.pallas_call(
        functools.partial(kernel, shards, chans, chunks, parts, group, many),
        out_shape=jax.ShapeDtypeStruct((count, width), BF16),
        in_specs=[pl.BlockSpec(memory_space=pl.ANY)] * len(operands),
        out_specs=pl.BlockSpec(memory_space=vmem),
        scratch_shapes=[
            vmem((chans, count, width), BF16),
            vmem((chans, RIM, width), BF16),
            vmem((inputs, wide), BF16),
            vmem(short_filter.shape, F32),
            vmem((count, width), F32),
            vmem((1, width), F32),
        ] + [vmem(c.shape, F32) for c in consts] + [
            vmem(outer.shape, BF16),
            vmem((2,) + ahead.shape, BF16),
            vmem((2,) + back.shape, BF16),
            vmem((2,) + close.shape, BF16),
            vmem((RIM + count, wide), F32),
            vmem((RIM, wide), BF16),
            vmem((RIM, wide), BF16),
            vmem((count, width), F32),
            vmem((blocks * LANES, LANES), F32),
            vmem((blocks * LANES, LANES), F32),
            vmem(swap_shape, F32),
            vmem(filter_shape, F32),
            vmem(filter_shape, BF16),
            vmem(filter_shape, BF16),
            vmem(swap_shape, BF16),
            vmem(swap_shape, BF16),
            vmem(back_shape, BF16),
            vmem(back_shape, BF16),
            vmem(flat_shape, F32),
            vmem((shards * many * blocks, LANES), F32),
            vmem((cd // many, many * turn.shape[1], 2 * LANES), F32),
            vmem(back_shape[1:], F32),
            vmem((shards * group * blocks, LANES), F32),
            vmem((chans, groups, group * shards, count), BF16),
            vmem((chans, width, LANES), BF16),
            vmem((width, LANES), F32),
            vmem((groups, chans, group * shards, LANES), F32),
            vmem((groups, LANES, chans * group * shards), BF16),
            vmem((LANES, count), F32),
            vmem((LANES, LANES), F32),
            dma((14,)),
            dma((2, chunks + 1)), dma((chans, chunks + 1)), dma((chunks + 1,)),
            dma((3,)), dma((chans,)), dma, dma,
            dma((cd // many,)), dma((cd // many,)),
            dma((parts,)), dma((parts,)),
            dma((groups,)), dma((groups,)),
            dma((2, groups)), dma((chans, groups)), dma((groups,)),
        ],
        compiler_params=pltpu.CompilerParams(
            collective_id=0, has_side_effects=True, vmem_limit_bytes=56 * 1024 * 1024
        ),
        cost_estimate=pl.CostEstimate(flops=4 * 10**9, bytes_accessed=4 * 10**6, transcendentals=0),
    )(*operands)


def solution(mesh):
    shards, chans = mesh.shape["seq"], mesh.shape["chan"]
    return jax.shard_map(
        functools.partial(on_device, shards, chans),
        mesh=mesh,
        in_specs=(
            P("seq", "chan"),
            P(None, None, "chan"),
            P(None, None, "chan"),
            P("seq", "chan"),
            P("chan"),
            P("chan", None),
        ),
        out_specs=P("seq", "chan"),
        check_vma=False,
    )
```

```python
import functools
import math

import jax
import jax.numpy as jnp
import numpy as np
from jax import lax
from jax.experimental import pallas as pl
from jax.experimental.pallas import tpu as pltpu
from jax.sharding import PartitionSpec as P

MESH = pl.DeviceIdType.MESH
LANES = 128
RIM = 16
F32 = jnp.float32
BF16 = jnp.bfloat16


def split(values):
    high = values.astype(BF16)
    low = (values - high.astype(F32)).astype(BF16)
    return high, low


def split_table(table):
    table = np.asarray(table, np.float64)
    high = table.astype(np.float32).astype(BF16)
    low = (table - high.astype(np.float64)).astype(np.float32).astype(BF16)
    return high, low


def tables(total):
    first = total // LANES
    half = first // 2
    kept = half + 1
    padded = -(-kept // 16) * 16
    k1 = np.arange(padded)
    live = (k1 < kept).astype(np.float64)[:, None]
    n1 = np.arange(half)
    angle = 2.0 * math.pi / first * (k1[:, None] * n1[None, :] % first)
    outer = np.concatenate([np.cos(angle) * live, -np.sin(angle) * live], axis=0)
    outer_table = np.concatenate(split_table(outer), axis=1).astype(np.float32)
    n2 = np.arange(LANES)
    turn = 2.0 * math.pi / total * (k1[:, None] * n2[None, :] % total)
    turn_table = np.stack([np.cos(turn), -np.sin(turn)]).astype(np.float32)
    inner = 2.0 * math.pi / LANES * (n2[:, None] * n2[None, :] % LANES)
    cosine, sine = np.cos(inner), -np.sin(inner)
    ahead = np.block([[cosine, sine], [-sine, cosine]])
    ahead_table = ahead.astype(np.float32)
    back_table = ahead.T.astype(np.float32)
    weight = np.where((k1 == 0) | (k1 == half), 1.0, 2.0) * live[:, 0] / total
    close = np.concatenate([np.cos(angle).T * weight, -np.sin(angle).T * weight], axis=1)
    close_table = close.astype(np.float32)
    return outer_table, turn_table, ahead_table, back_table, close_table


def dot(left, right):
    return jnp.dot(left, right, preferred_element_type=F32)


def each(low, high, body):
    def one(i, carry):
        body(i)
        return carry

    lax.fori_loop(low, high, one, 0)


def piece(start, size):
    return pl.ds(pl.multiple_of(start, size), size)


def dot2(left, table_ref):
    rounded = left.astype(BF16)
    return dot(rounded, table_ref[0]) + dot(rounded, table_ref[1])


def kernel(
    shards, chans, chunks, parts, group, many,
    tok, w_in, sfilt_a, lfilt_a, gain_a, w_out, outer_a, turn_a, ahead_a, back_a, close_a,
    out,
    tbuf, tmini, w, sfilt, lfilt, gain, outer_f, turn_t, ahead_f, back_f, close_f,
    outer_t, ahead_t, back_t, close_t,
    proj, rim_out, rim_in, keep, keep_t, skip_t, stage, h_stage, hs, hr, xs, xr, ys, yr,
    x32, h32, hspec, y32, c32, gbuf, wbuf, w32, w_rows, wt, acc, gain_rows,
    local, tok_send, tok_recv, fwd_send, wo_send, wo_recv, rim_send, rim_recv,
    h_send, h_recv, x_send, x_recv, y_send, y_recv, g_send, g_recv, gf_send,
):
    seq = lax.axis_index("seq")
    chan = lax.axis_index("chan")
    count = tok.shape[0]
    blocks = count // LANES
    cd = LANES // shards
    groups = cd // group
    lots = cd // many
    per = many // group
    rows = count // chunks
    core_peer = chan + 1 - 2 * (chan % 2)
    x_peer = (chan + 2) % chans
    diag = (core_peer + 2) % chans
    others = (core_peer, x_peer, diag)
    far_first = sorted(range(1, shards), key=lambda d: -min(d, shards - d))

    own_columns = pl.ds(pl.multiple_of(chan * LANES, LANES), LANES)
    loads = [(lfilt_a, lfilt), (tok, tbuf.at[chan]), (tok.at[pl.ds(count - RIM, RIM)], tmini.at[chan])]
    loads += [(w_in.at[g], w.at[:, pl.ds(g * LANES, LANES)]) for g in range(3)]
    loads += [(sfilt_a, sfilt), (gain_a, gain), (w_out.at[:, own_columns], wbuf.at[chan])]
    loads += [(outer_a, outer_f), (turn_a, turn_t), (ahead_a, ahead_f), (back_a, back_f), (close_a, close_f)]
    copies = [pltpu.make_async_copy(src, dst, local.at[i]) for i, (src, dst) in enumerate(loads)]
    for copy in copies:
        copy.start()

    barrier = pltpu.get_barrier_semaphore()
    for peer in others:
        pl.semaphore_signal(barrier, inc=1, device_id=(seq, peer), device_id_type=MESH)

    @functools.partial(each, 1, shards)
    def greet(d):
        peer = (seq + d) % shards
        pl.semaphore_signal(barrier, inc=1, device_id=(peer, chan), device_id_type=MESH)

    def spread(turned, block):
        for dest in range(shards):
            stage[dest, piece(block * cd, cd), :] = turned[dest * cd:(dest + 1) * cd, :]

    def pack(dst, part, pieces):
        size = blocks // pieces * cd
        span = piece(part * size, size)
        dst[:, span, :] = stage[:, span, :].astype(BF16)

    copies[0].wait()
    @functools.partial(each, 0, blocks)
    def spread_filter(block):
        turned = lfilt[piece(block * LANES, LANES), :].T
        for dest in range(shards):
            for g in range(lots):
                start = dest * cd + g * many
                h_stage[g, dest, piece(block * many, many), :] = turned[start:start + many, :]

    hs[...] = h_stage[...].astype(BF16)
    for copy in copies[1:]:
        copy.wait()
    gain_rows[...] = jnp.broadcast_to(gain[...], (LANES, LANES)).T
    outer_t[...] = outer_f[...].astype(BF16)
    for table, ref in ((ahead_f, ahead_t), (back_f, back_t), (close_f, close_t)):
        high, low = split(table[...])
        ref[0] = high
        ref[1] = low
    pl.semaphore_wait(barrier, len(others) + shards - 1)

    def remote(src, dst, send, recv, device):
        return pltpu.make_async_remote_copy(
            src_ref=src, dst_ref=dst, send_sem=send, recv_sem=recv,
            device_id=device, device_id_type=MESH,
        )

    def first(k):
        return isinstance(k, int) and k == 0

    def landing(k, owner):
        if first(k):
            return tmini.at[owner]
        return tbuf.at[owner, piece((k - 1) * rows, rows)]

    def tok_copy(k, slot, peer, owner):
        span = pl.ds(count - RIM, RIM) if first(k) else piece((k - 1) * rows, rows)
        return remote(tok.at[span], landing(k, owner), tok_send.at[slot, k], tok_recv.at[owner, k], (seq, peer))

    def fwd_copy(k, owner):
        return remote(landing(k, owner), landing(k, owner), fwd_send.at[k], tok_recv.at[owner, k], (seq, core_peer))

    def give(k):
        tok_copy(k, 1, x_peer, chan).start()
        tok_copy(k, 0, core_peer, chan).start()

    give(0)
    each(1, chunks + 1, give)

    def wo_copy(slot, peer, owner):
        columns = pl.ds(pl.multiple_of(peer * LANES, LANES), LANES)
        return remote(w_out.at[:, columns], wbuf.at[owner], wo_send.at[slot], wo_recv.at[owner], (seq, peer))

    def swap_all(action, src, dst, send, recv, part, span):
        if action == "start":
            for d in far_first:
                peer = (seq + d) % shards
                remote(src.at[peer, span], dst.at[seq, span], send.at[part], recv.at[part], (peer, chan)).start()
            return
        several = pl.ds(0, shards - 1)
        whole = remote(
            src.at[several, span], dst.at[several, span], send.at[part], recv.at[part], ((seq + 1) % shards, chan)
        )
        if action == "recv":
            whole.wait_recv()
        else:
            whole.wait_send()

    def h_swap(action, g):
        swap_all(action, hs.at[g], hr.at[g], h_send, h_recv, g, pl.ds(0, blocks * many))

    def x_swap(action, part):
        size = blocks // parts * cd
        swap_all(action, xs, xr, x_send, x_recv, part, piece(part * size, size))

    def y_swap(action, g):
        swap_all(action, ys.at[g], yr.at[g], y_send, y_recv, g, pl.ds(0, group * blocks))

    h_swap("start", 0)
    for g in range(lots):
        hr[g, seq] = hs[g, seq]
    for slot, peer in enumerate(others):
        wo_copy(slot, peer, chan).start()

    def shorten(k):
        for g in range(3):
            lanes = slice(g * LANES, (g + 1) * LANES)
            base = pl.multiple_of(RIM // 2 + k * rows, 8)
            window = proj[pl.ds(base, rows + 8), lanes]
            value = (
                sfilt[0, g:g + 1, :] * window[8:, :]
                + sfilt[1, g:g + 1, :] * window[7:-1, :]
                + sfilt[2, g:g + 1, :] * window[6:-2, :]
            )
            if g == 0:
                held = value
            elif g == 1:
                held = held * value
            else:
                keep[piece(k * rows, rows), :] = value
        for j in range(rows // LANES):
            block = k * (rows // LANES) + j
            turned = held[j * LANES:(j + 1) * LANES, :].T
            spread(turned, block)
            skip_t[piece(block * LANES, LANES), :] = turned * gain_rows[...]

    def rim_copy():
        return remote(rim_out, rim_in, rim_send, rim_recv, ((seq + 1) % shards, chan))

    def lead(k):
        tok_copy(k, 1, x_peer, x_peer).wait_recv()
        fwd_copy(k, x_peer).start()

    def take(k):
        tok_copy(k, 0, core_peer, core_peer).wait_recv()
        tok_copy(k, 0, core_peer, diag).wait_recv()

    lead(0)
    take(0)
    tail = jnp.concatenate([tmini[j] for j in range(chans)], axis=1)
    rim_out[...] = dot(tail, w[...]).astype(BF16)
    rim_copy().start()
    lead(1)
    @functools.partial(each, 0, parts)
    def project(part):
        for i in range(chunks // parts):
            k = part * (chunks // parts) + i
            pl.when(k + 1 < chunks)(lambda: lead(k + 2))
            take(k + 1)
            span = piece(k * rows, rows)
            features = jnp.concatenate([tbuf[j, span, :] for j in range(chans)], axis=1)
            projected = dot(features, w[...]).astype(BF16)
            proj[pl.ds(pl.multiple_of(RIM + k * rows, RIM), rows), :] = projected.astype(F32)
            if i == 0:
                @pl.when(part == 0)
                def edge_rows():
                    rim_copy().wait_recv()
                    live = (seq > 0).astype(F32)
                    proj[0:RIM, :] = rim_in[...].astype(F32) * live
            shorten(k)
        pack(xs, part, parts)
        x_swap("start", part)
        for j in range(blocks // parts):
            span = piece((part * (blocks // parts) + j) * LANES, LANES)
            keep_t[span, :] = keep[span, :].T

    for g in range(1, lots):
        h_swap("start", g)
    xr[seq] = xs[seq]

    height = shards * blocks
    padded = turn_t.shape[1]
    edge = group * padded

    def spectrum(ref, start, size, stride, product):
        columns = [ref[pl.ds(start + j, height, stride=stride), :].astype(BF16) for j in range(size)]
        signal = jnp.concatenate(columns, axis=1)
        signal = jnp.concatenate([signal, signal], axis=0)
        opened = dot(outer_t[...], signal)
        cosine, sine = turn_t[0], turn_t[1]
        turned = []
        for j in range(size):
            real = opened[:padded, j * LANES:(j + 1) * LANES]
            imag = opened[padded:, j * LANES:(j + 1) * LANES]
            turned.append(jnp.concatenate([real * cosine - imag * sine, real * sine + imag * cosine], axis=1))
        return product(jnp.concatenate(turned, axis=0), ahead_t)

    def dot1(left, table_ref):
        return dot(left.astype(BF16), table_ref[0])

    def filter_spectra(g):
        h_swap("recv", g)
        h32[...] = hr[g].reshape(h32.shape).astype(F32)
        hspec[g] = spectrum(h32, 0, many, many, dot2)

    filter_spectra(0)
    acc[...] = jnp.zeros_like(acc)

    for part in range(parts):
        x_swap("recv", part)
    x32[...] = xr[...].reshape(x32.shape).astype(F32)

    def convolve(g):
        spectra = spectrum(x32, g * group, group, cd, dot1)
        xr_, xi_ = spectra[:, :LANES], spectra[:, LANES:]
        at = piece(g % per * edge, edge)
        hr_, hi_ = hspec[g // per, at, :LANES], hspec[g // per, at, LANES:]
        product = jnp.concatenate([xr_ * hr_ - xi_ * hi_, xr_ * hi_ + xi_ * hr_], axis=1)
        back = dot1(product, back_t)
        cosine, sine = turn_t[0], turn_t[1]
        sums = []
        for j in range(group):
            real = back[j * padded:(j + 1) * padded, :LANES]
            imag = back[j * padded:(j + 1) * padded, LANES:]
            sums.append(jnp.concatenate([real * cosine + imag * sine, imag * cosine - real * sine], axis=0))
        conv = dot(close_t[0], jnp.concatenate(sums, axis=1).astype(BF16))
        for j in range(group):
            y32[:, j * blocks:(j + 1) * blocks, :] = conv[:, j * LANES:(j + 1) * LANES].reshape(shards, blocks, LANES)
        ys[g] = y32[...].astype(BF16)
        y_swap("start", g)
        yr[g, seq] = ys[g, seq]

    def gated_copy(g, slot, peer, owner):
        return remote(gbuf.at[chan, g], gbuf.at[owner, g], g_send.at[slot, g], g_recv.at[owner, g], (seq, peer))

    def gated_fwd(g, owner):
        return remote(gbuf.at[owner, g], gbuf.at[owner, g], gf_send.at[g], g_recv.at[owner, g], (seq, core_peer))

    def gate(g):
        y_swap("recv", g)
        c32[...] = yr[g].reshape(c32.shape).astype(F32)
        for block in range(blocks):
            pieces = []
            for c in range(group):
                conv = c32[pl.ds(c * blocks + block, shards, stride=group * blocks), :]
                at = pl.ds(block * LANES + g * group + c, shards, stride=cd)
                pieces.append(keep_t[at, :] * (conv + skip_t[at, :]))
            gbuf[chan, g, :, block * LANES:(block + 1) * LANES] = jnp.concatenate(pieces, axis=0).astype(BF16)
        gated_copy(g, 1, x_peer, chan).start()
        gated_copy(g, 0, core_peer, chan).start()

    def forward(g):
        gated_copy(g, 1, x_peer, x_peer).wait_recv()
        gated_fwd(g, x_peer).start()

    def mix(g):
        gated_copy(g, 0, core_peer, core_peer).wait_recv()
        gated_copy(g, 0, core_peer, diag).wait_recv()
        whole = jnp.concatenate([gbuf[j, g] for j in range(chans)], axis=0)
        acc[...] += dot(wt[g], whole)

    def meanwhile():
        for slot, peer in enumerate(others):
            wo_copy(slot, peer, peer).wait_recv()

        @functools.partial(each, 0, chans)
        def turn_weights(j):
            w32[...] = wbuf[j].astype(F32)
            for g in range(groups):
                picked = [w32[pl.ds(g * group + c, shards, stride=cd), :] for c in range(group)]
                w_rows[g, j] = jnp.concatenate(picked, axis=0)

        @functools.partial(each, 0, groups)
        def pack_weights(g):
            wt[g] = jnp.concatenate([w_rows[g, j] for j in range(chans)], axis=0).T.astype(BF16)

        def settle(k):
            tok_copy(k, 1, x_peer, chan).wait_send()
            tok_copy(k, 0, core_peer, chan).wait_send()
            fwd_copy(k, x_peer).wait_send()

        settle(0)
        each(1, chunks + 1, settle)
        for slot, peer in enumerate(others):
            wo_copy(slot, peer, chan).wait_send()
        rim_copy().wait_send()
        each(0, lots, lambda g: h_swap("send", g))

    @functools.partial(each, 0, groups + 1)
    def stream(g):
        pl.when((g >= 1) & (g < groups) & (g % per == 0))(lambda: filter_spectra(g // per))
        pl.when(g < groups)(lambda: convolve(g))
        pl.when(g >= 2)(lambda: forward(g - 2))
        pl.when(g >= 1)(lambda: gate(g - 1))
        pl.when(g == groups - 1)(meanwhile)
        pl.when(g >= 3)(lambda: mix(g - 3))

    forward(groups - 1)
    each(0, parts, lambda part: x_swap("send", part))
    each(0, groups, lambda g: y_swap("send", g))
    each(max(groups - 2, 0), groups, mix)
    for block in range(blocks):
        span = slice(block * LANES, (block + 1) * LANES)
        out[span, :] = acc[:, span].T.astype(BF16)

    @functools.partial(each, 0, groups)
    def finish(g):
        gated_copy(g, 1, x_peer, chan).wait_send()
        gated_copy(g, 0, core_peer, chan).wait_send()
        gated_fwd(g, x_peer).wait_send()


def on_device(shards, chans, tokens, w_in, short_filter, long_filter, skip_gain, w_out):
    count, width = tokens.shape
    length = shards * count
    blocks = count // LANES
    cd = width // shards
    chunks = 4
    parts = 4 if blocks // 4 * cd % 16 == 0 else 2
    group = min(cd, 8)
    many = min(cd, 8)
    groups = cd // group
    consts = tables(2 * length)
    outer, turn, ahead, back, close = consts
    wide = 3 * width
    inputs = w_in.shape[0]
    dma = pltpu.SemaphoreType.DMA
    vmem = pltpu.VMEM
    swap_shape = (shards, blocks * cd, LANES)
    flat_shape = (shards * blocks * cd, LANES)
    back_shape = (groups, shards, group * blocks, LANES)
    filter_shape = (cd // many, shards, many * blocks, LANES)
    operands = (
        tokens, w_in.transpose(1, 0, 2), short_filter, long_filter,
        skip_gain.reshape(1, width), w_out,
    ) + tuple(jnp.asarray(c) for c in consts)
    return pl.pallas_call(
        functools.partial(kernel, shards, chans, chunks, parts, group, many),
        out_shape=jax.ShapeDtypeStruct((count, width), BF16),
        in_specs=[pl.BlockSpec(memory_space=pl.ANY)] * len(operands),
        out_specs=pl.BlockSpec(memory_space=vmem),
        scratch_shapes=[
            vmem((chans, count, width), BF16),
            vmem((chans, RIM, width), BF16),
            vmem((inputs, wide), BF16),
            vmem(short_filter.shape, F32),
            vmem((count, width), F32),
            vmem((1, width), F32),
        ] + [vmem(c.shape, F32) for c in consts] + [
            vmem(outer.shape, BF16),
            vmem((2,) + ahead.shape, BF16),
            vmem((2,) + back.shape, BF16),
            vmem((2,) + close.shape, BF16),
            vmem((RIM + count, wide), F32),
            vmem((RIM, wide), BF16),
            vmem((RIM, wide), BF16),
            vmem((count, width), F32),
            vmem((blocks * LANES, LANES), F32),
            vmem((blocks * LANES, LANES), F32),
            vmem(swap_shape, F32),
            vmem(filter_shape, F32),
            vmem(filter_shape, BF16),
            vmem(filter_shape, BF16),
            vmem(swap_shape, BF16),
            vmem(swap_shape, BF16),
            vmem(back_shape, BF16),
            vmem(back_shape, BF16),
            vmem(flat_shape, F32),
            vmem((shards * many * blocks, LANES), F32),
            vmem((cd // many, many * turn.shape[1], 2 * LANES), F32),
            vmem(back_shape[1:], F32),
            vmem((shards * group * blocks, LANES), F32),
            vmem((chans, groups, group * shards, count), BF16),
            vmem((chans, width, LANES), BF16),
            vmem((width, LANES), F32),
            vmem((groups, chans, group * shards, LANES), F32),
            vmem((groups, LANES, chans * group * shards), BF16),
            vmem((LANES, count), F32),
            vmem((LANES, LANES), F32),
            dma((14,)),
            dma((2, chunks + 1)), dma((chans, chunks + 1)), dma((chunks + 1,)),
            dma((3,)), dma((chans,)), dma, dma,
            dma((cd // many,)), dma((cd // many,)),
            dma((parts,)), dma((parts,)),
            dma((groups,)), dma((groups,)),
            dma((2, groups)), dma((chans, groups)), dma((groups,)),
        ],
        compiler_params=pltpu.CompilerParams(
            collective_id=0, has_side_effects=True, vmem_limit_bytes=56 * 1024 * 1024
        ),
        cost_estimate=pl.CostEstimate(flops=4 * 10**9, bytes_accessed=4 * 10**6, transcendentals=0),
    )(*operands)


def solution(mesh):
    shards, chans = mesh.shape["seq"], mesh.shape["chan"]
    return jax.shard_map(
        functools.partial(on_device, shards, chans),
        mesh=mesh,
        in_specs=(
            P("seq", "chan"),
            P(None, None, "chan"),
            P(None, None, "chan"),
            P("seq", "chan"),
            P("chan"),
            P("chan", None),
        ),
        out_specs=P("seq", "chan"),
        check_vma=False,
    )
```

```python
import functools
import math

import jax
import jax.numpy as jnp
import numpy as np
from jax import lax
from jax.experimental import pallas as pl
from jax.experimental.pallas import tpu as pltpu
from jax.sharding import PartitionSpec as P

MESH = pl.DeviceIdType.MESH
LANES = 128
RIM = 16
F32 = jnp.float32
BF16 = jnp.bfloat16


def split(values):
    high = values.astype(BF16)
    low = (values - high.astype(F32)).astype(BF16)
    return high, low


def split_table(table):
    table = np.asarray(table, np.float64)
    high = table.astype(np.float32).astype(BF16)
    low = (table - high.astype(np.float64)).astype(np.float32).astype(BF16)
    return high, low


def tables(total):
    first = total // LANES
    half = first // 2
    kept = half + 1
    padded = -(-kept // 16) * 16
    k1 = np.arange(padded)
    live = (k1 < kept).astype(np.float64)[:, None]
    n1 = np.arange(half)
    angle = 2.0 * math.pi / first * (k1[:, None] * n1[None, :] % first)
    outer = np.concatenate([np.cos(angle) * live, -np.sin(angle) * live], axis=0)
    outer_table = np.concatenate(split_table(outer), axis=1).astype(np.float32)
    n2 = np.arange(LANES)
    turn = 2.0 * math.pi / total * (k1[:, None] * n2[None, :] % total)
    turn_table = np.stack([np.cos(turn), -np.sin(turn)]).astype(np.float32)
    inner = 2.0 * math.pi / LANES * (n2[:, None] * n2[None, :] % LANES)
    cosine, sine = np.cos(inner), -np.sin(inner)
    ahead = np.block([[cosine, sine], [-sine, cosine]])
    ahead_table = ahead.astype(np.float32)
    back_table = ahead.T.astype(np.float32)
    weight = np.where((k1 == 0) | (k1 == half), 1.0, 2.0) * live[:, 0] / total
    close = np.concatenate([np.cos(angle).T * weight, -np.sin(angle).T * weight], axis=1)
    close_table = close.astype(np.float32)
    return outer_table, turn_table, ahead_table, back_table, close_table


def dot(left, right):
    return jnp.dot(left, right, preferred_element_type=F32)


def each(low, high, body):
    def one(i, carry):
        body(i)
        return carry

    lax.fori_loop(low, high, one, 0)


def piece(start, size):
    return pl.ds(pl.multiple_of(start, size), size)


def dot2(left, table_ref):
    rounded = left.astype(BF16)
    return dot(rounded, table_ref[0]) + dot(rounded, table_ref[1])


def kernel(
    shards, chans, chunks, parts, group, many,
    tok, w_in, sfilt_a, lfilt_a, gain_a, w_out, outer_a, turn_a, ahead_a, back_a, close_a,
    out,
    tbuf, tmini, w, sfilt, lfilt, gain, outer_f, turn_t, ahead_f, back_f, close_f,
    outer_t, ahead_t, back_t, close_t,
    proj, rim_out, rim_in, keep, keep_t, skip_t, stage, h_stage, hs, hr, xs, xr, ys, yr,
    x32, h32, hspec, y32, c32, gbuf, wbuf, w32, w_rows, wt, acc, gain_rows,
    local, tok_send, tok_recv, fwd_send, wo_send, wo_recv, rim_send, rim_recv,
    h_send, h_recv, x_send, x_recv, y_send, y_recv, g_send, g_recv, gf_send,
):
    seq = lax.axis_index("seq")
    chan = lax.axis_index("chan")
    count = tok.shape[0]
    blocks = count // LANES
    cd = LANES // shards
    groups = cd // group
    lots = cd // many
    per = many // group
    rows = count // chunks
    core_peer = chan + 1 - 2 * (chan % 2)
    x_peer = (chan + 2) % chans
    diag = (core_peer + 2) % chans
    others = (core_peer, x_peer, diag)
    far_first = sorted(range(1, shards), key=lambda d: -min(d, shards - d))

    own_columns = pl.ds(pl.multiple_of(chan * LANES, LANES), LANES)
    loads = [(lfilt_a, lfilt), (tok, tbuf.at[chan]), (tok.at[pl.ds(count - RIM, RIM)], tmini.at[chan])]
    loads += [(w_in.at[g], w.at[:, pl.ds(g * LANES, LANES)]) for g in range(3)]
    loads += [(sfilt_a, sfilt), (gain_a, gain), (w_out.at[:, own_columns], wbuf.at[chan])]
    loads += [(outer_a, outer_f), (turn_a, turn_t), (ahead_a, ahead_f), (back_a, back_f), (close_a, close_f)]
    copies = [pltpu.make_async_copy(src, dst, local.at[i]) for i, (src, dst) in enumerate(loads)]
    for copy in copies:
        copy.start()

    barrier = pltpu.get_barrier_semaphore()
    for peer in others:
        pl.semaphore_signal(barrier, inc=1, device_id=(seq, peer), device_id_type=MESH)

    @functools.partial(each, 1, shards)
    def greet(d):
        peer = (seq + d) % shards
        pl.semaphore_signal(barrier, inc=1, device_id=(peer, chan), device_id_type=MESH)

    def spread(turned, block):
        for dest in range(shards):
            stage[dest, piece(block * cd, cd), :] = turned[dest * cd:(dest + 1) * cd, :]

    def pack(dst, part, pieces):
        size = blocks // pieces * cd
        span = piece(part * size, size)
        dst[:, span, :] = stage[:, span, :].astype(BF16)

    copies[0].wait()
    @functools.partial(each, 0, blocks)
    def spread_filter(block):
        turned = lfilt[piece(block * LANES, LANES), :].T
        for dest in range(shards):
            for g in range(lots):
                start = dest * cd + g * many
                h_stage[g, dest, piece(block * many, many), :] = turned[start:start + many, :]

    hs[...] = h_stage[...].astype(BF16)
    for copy in copies[1:]:
        copy.wait()
    gain_rows[...] = jnp.broadcast_to(gain[...], (LANES, LANES)).T
    outer_t[...] = outer_f[...].astype(BF16)
    for table, ref in ((ahead_f, ahead_t), (back_f, back_t), (close_f, close_t)):
        high, low = split(table[...])
        ref[0] = high
        ref[1] = low
    pl.semaphore_wait(barrier, len(others) + shards - 1)

    def remote(src, dst, send, recv, device):
        return pltpu.make_async_remote_copy(
            src_ref=src, dst_ref=dst, send_sem=send, recv_sem=recv,
            device_id=device, device_id_type=MESH,
        )

    def first(k):
        return isinstance(k, int) and k == 0

    def landing(k, owner):
        if first(k):
            return tmini.at[owner]
        return tbuf.at[owner, piece((k - 1) * rows, rows)]

    def tok_copy(k, slot, peer, owner):
        span = pl.ds(count - RIM, RIM) if first(k) else piece((k - 1) * rows, rows)
        return remote(tok.at[span], landing(k, owner), tok_send.at[slot, k], tok_recv.at[owner, k], (seq, peer))

    def fwd_copy(k, owner):
        return remote(landing(k, owner), landing(k, owner), fwd_send.at[k], tok_recv.at[owner, k], (seq, core_peer))

    def give(k):
        tok_copy(k, 1, x_peer, chan).start()
        tok_copy(k, 0, core_peer, chan).start()

    give(0)
    each(1, chunks + 1, give)

    def wo_copy(slot, peer, owner):
        columns = pl.ds(pl.multiple_of(peer * LANES, LANES), LANES)
        return remote(w_out.at[:, columns], wbuf.at[owner], wo_send.at[slot], wo_recv.at[owner], (seq, peer))

    def swap_all(action, src, dst, send, recv, part, span):
        if action == "start":
            for d in far_first:
                peer = (seq + d) % shards
                remote(src.at[peer, span], dst.at[seq, span], send.at[part], recv.at[part], (peer, chan)).start()
            return
        several = pl.ds(0, shards - 1)
        whole = remote(
            src.at[several, span], dst.at[several, span], send.at[part], recv.at[part], ((seq + 1) % shards, chan)
        )
        if action == "recv":
            whole.wait_recv()
        else:
            whole.wait_send()

    def h_swap(action, g):
        swap_all(action, hs.at[g], hr.at[g], h_send, h_recv, g, pl.ds(0, blocks * many))

    def x_swap(action, part):
        size = blocks // parts * cd
        swap_all(action, xs, xr, x_send, x_recv, part, piece(part * size, size))

    def y_swap(action, g):
        swap_all(action, ys.at[g], yr.at[g], y_send, y_recv, g, pl.ds(0, group * blocks))

    h_swap("start", 0)
    for g in range(lots):
        hr[g, seq] = hs[g, seq]
    for slot, peer in enumerate(others):
        wo_copy(slot, peer, chan).start()

    def shorten(k):
        for g in range(3):
            lanes = slice(g * LANES, (g + 1) * LANES)
            base = pl.multiple_of(RIM // 2 + k * rows, 8)
            window = proj[pl.ds(base, rows + 8), lanes]
            value = (
                sfilt[0, g:g + 1, :] * window[8:, :]
                + sfilt[1, g:g + 1, :] * window[7:-1, :]
                + sfilt[2, g:g + 1, :] * window[6:-2, :]
            )
            if g == 0:
                held = value
            elif g == 1:
                held = held * value
            else:
                keep[piece(k * rows, rows), :] = value
        for j in range(rows // LANES):
            block = k * (rows // LANES) + j
            turned = held[j * LANES:(j + 1) * LANES, :].T
            spread(turned, block)
            skip_t[piece(block * LANES, LANES), :] = turned * gain_rows[...]

    def rim_copy():
        return remote(rim_out, rim_in, rim_send, rim_recv, ((seq + 1) % shards, chan))

    def lead(k):
        tok_copy(k, 1, x_peer, x_peer).wait_recv()
        fwd_copy(k, x_peer).start()

    def take(k):
        tok_copy(k, 0, core_peer, core_peer).wait_recv()
        tok_copy(k, 0, core_peer, diag).wait_recv()

    lead(0)
    take(0)
    tail = jnp.concatenate([tmini[j] for j in range(chans)], axis=1)
    rim_out[...] = dot(tail, w[...]).astype(BF16)
    rim_copy().start()
    lead(1)
    @functools.partial(each, 0, parts)
    def project(part):
        for i in range(chunks // parts):
            k = part * (chunks // parts) + i
            pl.when(k + 1 < chunks)(lambda: lead(k + 2))
            take(k + 1)
            span = piece(k * rows, rows)
            features = jnp.concatenate([tbuf[j, span, :] for j in range(chans)], axis=1)
            projected = dot(features, w[...]).astype(BF16)
            proj[pl.ds(pl.multiple_of(RIM + k * rows, RIM), rows), :] = projected.astype(F32)
            if i == 0:
                @pl.when(part == 0)
                def edge_rows():
                    rim_copy().wait_recv()
                    live = (seq > 0).astype(F32)
                    proj[0:RIM, :] = rim_in[...].astype(F32) * live
            shorten(k)
        pack(xs, part, parts)
        x_swap("start", part)
        for j in range(blocks // parts):
            span = piece((part * (blocks // parts) + j) * LANES, LANES)
            keep_t[span, :] = keep[span, :].T

    for g in range(1, lots):
        h_swap("start", g)
    xr[seq] = xs[seq]

    height = shards * blocks
    padded = turn_t.shape[1]
    edge = group * padded

    def spectrum(ref, start, size, stride, product):
        columns = [ref[pl.ds(start + j, height, stride=stride), :].astype(BF16) for j in range(size)]
        signal = jnp.concatenate(columns, axis=1)
        signal = jnp.concatenate([signal, signal], axis=0)
        opened = dot(outer_t[...], signal)
        cosine, sine = turn_t[0], turn_t[1]
        turned = []
        for j in range(size):
            real = opened[:padded, j * LANES:(j + 1) * LANES]
            imag = opened[padded:, j * LANES:(j + 1) * LANES]
            turned.append(jnp.concatenate([real * cosine - imag * sine, real * sine + imag * cosine], axis=1))
        return product(jnp.concatenate(turned, axis=0), ahead_t)

    def dot1(left, table_ref):
        return dot(left.astype(BF16), table_ref[0])

    def filter_spectra(g):
        h_swap("recv", g)
        h32[...] = hr[g].reshape(h32.shape).astype(F32)
        hspec[g] = spectrum(h32, 0, many, many, dot2)

    filter_spectra(0)
    acc[...] = jnp.zeros_like(acc)

    for part in range(parts):
        x_swap("recv", part)
    x32[...] = xr[...].reshape(x32.shape).astype(F32)

    def convolve(g):
        spectra = spectrum(x32, g * group, group, cd, dot1)
        xr_, xi_ = spectra[:, :LANES], spectra[:, LANES:]
        at = piece(g % per * edge, edge)
        hr_, hi_ = hspec[g // per, at, :LANES], hspec[g // per, at, LANES:]
        product = jnp.concatenate([xr_ * hr_ - xi_ * hi_, xr_ * hi_ + xi_ * hr_], axis=1)
        back = dot1(product, back_t)
        cosine, sine = turn_t[0], turn_t[1]
        sums = []
        for j in range(group):
            real = back[j * padded:(j + 1) * padded, :LANES]
            imag = back[j * padded:(j + 1) * padded, LANES:]
            sums.append(jnp.concatenate([real * cosine + imag * sine, imag * cosine - real * sine], axis=0))
        conv = dot(close_t[0], jnp.concatenate(sums, axis=1).astype(BF16))
        for j in range(group):
            y32[:, j * blocks:(j + 1) * blocks, :] = conv[:, j * LANES:(j + 1) * LANES].reshape(shards, blocks, LANES)
        ys[g] = y32[...].astype(BF16)
        y_swap("start", g)
        yr[g, seq] = ys[g, seq]

    def gated_copy(g, slot, peer, owner):
        return remote(gbuf.at[chan, g], gbuf.at[owner, g], g_send.at[slot, g], g_recv.at[owner, g], (seq, peer))

    def gated_fwd(g, owner):
        return remote(gbuf.at[owner, g], gbuf.at[owner, g], gf_send.at[g], g_recv.at[owner, g], (seq, core_peer))

    def gate(g):
        y_swap("recv", g)
        c32[...] = yr[g].reshape(c32.shape).astype(F32)
        for block in range(blocks):
            pieces = []
            for c in range(group):
                conv = c32[pl.ds(c * blocks + block, shards, stride=group * blocks), :]
                at = pl.ds(block * LANES + g * group + c, shards, stride=cd)
                pieces.append(keep_t[at, :] * (conv + skip_t[at, :]))
            gbuf[chan, g, :, block * LANES:(block + 1) * LANES] = jnp.concatenate(pieces, axis=0).astype(BF16)
        gated_copy(g, 1, x_peer, chan).start()
        gated_copy(g, 0, core_peer, chan).start()

    def forward(g):
        gated_copy(g, 1, x_peer, x_peer).wait_recv()
        gated_fwd(g, x_peer).start()

    def mix(g):
        gated_copy(g, 0, core_peer, core_peer).wait_recv()
        gated_copy(g, 0, core_peer, diag).wait_recv()
        whole = jnp.concatenate([gbuf[j, g] for j in range(chans)], axis=0)
        acc[...] += dot(wt[g], whole)

    def meanwhile():
        for slot, peer in enumerate(others):
            wo_copy(slot, peer, peer).wait_recv()

        @functools.partial(each, 0, chans)
        def turn_weights(j):
            w32[...] = wbuf[j].astype(F32)
            for g in range(groups):
                picked = [w32[pl.ds(g * group + c, shards, stride=cd), :] for c in range(group)]
                w_rows[g, j] = jnp.concatenate(picked, axis=0)

        @functools.partial(each, 0, groups)
        def pack_weights(g):
            wt[g] = jnp.concatenate([w_rows[g, j] for j in range(chans)], axis=0).T.astype(BF16)

        def settle(k):
            tok_copy(k, 1, x_peer, chan).wait_send()
            tok_copy(k, 0, core_peer, chan).wait_send()
            fwd_copy(k, x_peer).wait_send()

        settle(0)
        each(1, chunks + 1, settle)
        for slot, peer in enumerate(others):
            wo_copy(slot, peer, chan).wait_send()
        rim_copy().wait_send()
        each(0, lots, lambda g: h_swap("send", g))

    @functools.partial(each, 0, groups + 1)
    def stream(g):
        pl.when((g >= 1) & (g < groups) & (g % per == 0))(lambda: filter_spectra(g // per))
        pl.when(g < groups)(lambda: convolve(g))
        pl.when(g >= 2)(lambda: forward(g - 2))
        pl.when(g >= 1)(lambda: gate(g - 1))
        pl.when(g == groups - 1)(meanwhile)
        pl.when(g >= 3)(lambda: mix(g - 3))

    forward(groups - 1)
    each(0, parts, lambda part: x_swap("send", part))
    each(0, groups, lambda g: y_swap("send", g))
    each(max(groups - 2, 0), groups, mix)
    for block in range(blocks):
        span = slice(block * LANES, (block + 1) * LANES)
        out[span, :] = acc[:, span].T.astype(BF16)

    @functools.partial(each, 0, groups)
    def finish(g):
        gated_copy(g, 1, x_peer, chan).wait_send()
        gated_copy(g, 0, core_peer, chan).wait_send()
        gated_fwd(g, x_peer).wait_send()


def on_device(shards, chans, tokens, w_in, short_filter, long_filter, skip_gain, w_out):
    count, width = tokens.shape
    length = shards * count
    blocks = count // LANES
    cd = width // shards
    chunks = 2
    parts = 2
    group = min(cd, 8)
    many = min(cd, 8)
    groups = cd // group
    consts = tables(2 * length)
    outer, turn, ahead, back, close = consts
    wide = 3 * width
    inputs = w_in.shape[0]
    dma = pltpu.SemaphoreType.DMA
    vmem = pltpu.VMEM
    swap_shape = (shards, blocks * cd, LANES)
    flat_shape = (shards * blocks * cd, LANES)
    back_shape = (groups, shards, group * blocks, LANES)
    filter_shape = (cd // many, shards, many * blocks, LANES)
    operands = (
        tokens, w_in.transpose(1, 0, 2), short_filter, long_filter,
        skip_gain.reshape(1, width), w_out,
    ) + tuple(jnp.asarray(c) for c in consts)
    return pl.pallas_call(
        functools.partial(kernel, shards, chans, chunks, parts, group, many),
        out_shape=jax.ShapeDtypeStruct((count, width), BF16),
        in_specs=[pl.BlockSpec(memory_space=pl.ANY)] * len(operands),
        out_specs=pl.BlockSpec(memory_space=vmem),
        scratch_shapes=[
            vmem((chans, count, width), BF16),
            vmem((chans, RIM, width), BF16),
            vmem((inputs, wide), BF16),
            vmem(short_filter.shape, F32),
            vmem((count, width), F32),
            vmem((1, width), F32),
        ] + [vmem(c.shape, F32) for c in consts] + [
            vmem(outer.shape, BF16),
            vmem((2,) + ahead.shape, BF16),
            vmem((2,) + back.shape, BF16),
            vmem((2,) + close.shape, BF16),
            vmem((RIM + count, wide), F32),
            vmem((RIM, wide), BF16),
            vmem((RIM, wide), BF16),
            vmem((count, width), F32),
            vmem((blocks * LANES, LANES), F32),
            vmem((blocks * LANES, LANES), F32),
            vmem(swap_shape, F32),
            vmem(filter_shape, F32),
            vmem(filter_shape, BF16),
            vmem(filter_shape, BF16),
            vmem(swap_shape, BF16),
            vmem(swap_shape, BF16),
            vmem(back_shape, BF16),
            vmem(back_shape, BF16),
            vmem(flat_shape, F32),
            vmem((shards * many * blocks, LANES), F32),
            vmem((cd // many, many * turn.shape[1], 2 * LANES), F32),
            vmem(back_shape[1:], F32),
            vmem((shards * group * blocks, LANES), F32),
            vmem((chans, groups, group * shards, count), BF16),
            vmem((chans, width, LANES), BF16),
            vmem((width, LANES), F32),
            vmem((groups, chans, group * shards, LANES), F32),
            vmem((groups, LANES, chans * group * shards), BF16),
            vmem((LANES, count), F32),
            vmem((LANES, LANES), F32),
            dma((14,)),
            dma((2, chunks + 1)), dma((chans, chunks + 1)), dma((chunks + 1,)),
            dma((3,)), dma((chans,)), dma, dma,
            dma((cd // many,)), dma((cd // many,)),
            dma((parts,)), dma((parts,)),
            dma((groups,)), dma((groups,)),
            dma((2, groups)), dma((chans, groups)), dma((groups,)),
        ],
        compiler_params=pltpu.CompilerParams(
            collective_id=0, has_side_effects=True, vmem_limit_bytes=56 * 1024 * 1024
        ),
        cost_estimate=pl.CostEstimate(flops=4 * 10**9, bytes_accessed=4 * 10**6, transcendentals=0),
    )(*operands)


def solution(mesh):
    shards, chans = mesh.shape["seq"], mesh.shape["chan"]
    return jax.shard_map(
        functools.partial(on_device, shards, chans),
        mesh=mesh,
        in_specs=(
            P("seq", "chan"),
            P(None, None, "chan"),
            P(None, None, "chan"),
            P("seq", "chan"),
            P("chan"),
            P("chan", None),
        ),
        out_specs=P("seq", "chan"),
        check_vma=False,
    )
```
